128 devices in a mesh: row: 8 (over x, core), col: 16 (over z, y).
Axes of the slice: x: 4, y: 4, z: 4, core: 2. Of those that a mesh axis runs over, the one named last changes fastest.
Arguments:
- flat_grad: bfloat16 [12288, 26624], P(('row', 'col')), may hold values from -6 to 6
- flat_rows: int32 [12288], P(('row', 'col')), may hold values from 0 to 12287, as said below
- momentum: bfloat16 [12288, 26624], P('row', 'col'), may hold values from -6 to 6
- basis: float32 [26624, 128], P('col'), may hold values from -0.0390625 to 0.0390625
Outputs:
- new_momentum: bfloat16 [12288, 26624], P('row', 'col')
- new_basis: float32 [26624, 128], P('col')
- flat_update: bfloat16 [12288, 26624], P(('row', 'col'))
The draws below stay inside these ranges and needn't reach their ends.
Inputs may be any that keep to these rules, and one draw needn't show every extreme that they name: Within each aligned block of 12288 / 8 flat rows, flat_rows is a permutation of the matrix rows of that same block.
All inputs are finite; a program needn't handle non-finite values.
Results may differ from the reference program's by a relative error of at most 0.028.
Values may be sent and summed in bfloat16 or wider, within the bound.
A program may use at most 128 MiB of HBM per device.

```python
import math
import jax
import jax.numpy as jnp
from jax import lax

ROWS = 12288
COLS = 26624
RANK = 128
ITERS = 4
N_ROW = 8


def row_order(key):
    key = jax.random.fold_in(key, 5)
    block = ROWS // N_ROW
    keys = jax.random.split(key, N_ROW)
    perms = jax.vmap(lambda k: jax.random.permutation(k, block))(keys)
    starts = jnp.arange(N_ROW, dtype=jnp.int32)[:, None] * block
    return (perms.astype(jnp.int32) + starts).reshape(ROWS).astype(jnp.int32)


def shared_factors(key):
    key = jax.random.fold_in(key, 11)
    key_left, key_right = jax.random.split(key)
    width = 2 * RANK
    left_f = jax.random.normal(key_left, (ROWS, width), jnp.float32)
    right_f = jax.random.normal(key_right, (COLS, width), jnp.float32)
    return (left_f, right_f)


def column_scale(ratio):
    steps = jnp.arange(COLS, dtype=jnp.float32) / (COLS - 1)
    return jnp.exp(jnp.log(ratio) * (steps - 0.5))


def combine(left_f, right_f, lowest, amplitude):
    width = left_f.shape[1]
    steps = jnp.arange(width, dtype=jnp.float32) / width
    weights = 1.0 - (1.0 - lowest) * steps
    weights = weights / jnp.sqrt(jnp.sum(weights * weights))
    return amplitude * jnp.dot(left_f * weights, right_f.T, precision=lax.Precision.HIGHEST)


def draw_flat_rows(key, part):
    order = row_order(key)
    return order


def draw_momentum(key, part):
    left_f, right_f = shared_factors(key)
    key = jax.random.fold_in(key, 7)
    noise = jax.random.normal(key, (ROWS, COLS), jnp.float32)
    lowest = 0.5
    amplitude = 1.0
    ratio = 4.0
    values = (combine(left_f, right_f, lowest, amplitude) + 0.6 * noise) * column_scale(ratio)[None, :]
    return jnp.clip(values, -6.0, 6.0).astype(jnp.bfloat16)


def draw_flat_grad(key, part):
    left_f, right_f = shared_factors(key)
    order = row_order(key)
    key = jax.random.fold_in(key, 9)
    noise = jax.random.normal(key, (ROWS, COLS), jnp.float32)
    lowest = 0.5
    amplitude = 0.5
    ratio = 4.0
    values = (combine(left_f[order], right_f, lowest, amplitude) + 0.8 * noise) * column_scale(ratio)[None, :]
    return jnp.clip(values, -6.0, 6.0).astype(jnp.bfloat16)


def level_of(stream_key, dims, pieces, least, high):
    level, own = 1.0, jax.random.fold_in(stream_key, 6)
    for position, shards_of in pieces:
        heights = jnp.exp(jax.random.uniform(jax.random.fold_in(own, position), (shards_of,), jnp.float32, least / len(pieces), high / len(pieces)))
        level = level * jnp.repeat(heights, dims[position] // shards_of).reshape([-1 if axis == position else 1 for axis in range(len(dims))])
    return level


def gaussian(rng, shape, spread, bound, shards=(), kind=jnp.bfloat16):
    result = spread * jax.random.normal(rng, shape, jnp.float32)
    if shards:
        result = result * level_of(rng, shape, shards, -0.22, 0.18)
    return jnp.clip(result, -bound, bound).astype(kind)


def setup_inputs(seed: int = 0) -> dict:
    streams_of = jax.random.split(jax.random.key(seed), 5)
    flat_grad = draw_flat_grad(jax.random.fold_in(streams_of[4], 71), 0)
    flat_rows = draw_flat_rows(jax.random.fold_in(streams_of[4], 71), 0)
    momentum = draw_momentum(jax.random.fold_in(streams_of[4], 71), 0)
    basis = gaussian(streams_of[3], (COLS, RANK), COLS ** -0.5, 0.0390625, ((0, 16),), jnp.float32)
    return {"flat_grad": flat_grad, "flat_rows": flat_rows, "momentum": momentum, "basis": basis}


def orthonormal(left):
    gram = jnp.dot(left.T.astype(jnp.float32), left.astype(jnp.float32), precision=lax.Precision.HIGHEST, preferred_element_type=jnp.float32)
    lower = jnp.linalg.cholesky(gram)
    return lax.linalg.triangular_solve(lower, left, left_side=False, lower=True, transpose_a=True)

def reference(flat_grad, flat_rows, momentum, basis):
    grad = jnp.zeros((ROWS, COLS), flat_grad.dtype).at[flat_rows].set(flat_grad)
    merged = (momentum.astype(jnp.float32) + grad.astype(jnp.float32)).astype(jnp.bfloat16)
    current = basis
    for step in range(ITERS):
        left = jnp.dot(merged.astype(jnp.float32), current.astype(jnp.bfloat16).astype(jnp.float32), preferred_element_type=jnp.float32)
        ortho = orthonormal(left).astype(jnp.bfloat16)
        right = jnp.einsum('mc,mr->cr', merged.astype(jnp.float32), ortho.astype(jnp.float32), preferred_element_type=jnp.float32)
        current = right / jnp.sqrt(lax.optimization_barrier(jnp.sum(right * right, axis=0)) + 1e-06)
    fed_back = jnp.dot(ortho.astype(jnp.float32), right.astype(jnp.bfloat16).T.astype(jnp.float32), preferred_element_type=jnp.float32)
    new_momentum = (merged.astype(jnp.float32) - 0.05 * fed_back).astype(jnp.bfloat16)
    factor = math.sqrt(ROWS * COLS / RANK)
    update = (factor * jnp.dot(ortho.astype(jnp.float32), current.astype(jnp.bfloat16).T.astype(jnp.float32), preferred_element_type=jnp.float32)).astype(jnp.bfloat16)
    return (new_momentum, current, update[flat_rows])
```

```python
import functools
import math

import jax
import jax.numpy as jnp
from jax import lax
from jax.experimental import pallas as pl
from jax.experimental.pallas import tpu as pltpu
from jax.sharding import PartitionSpec as P

ITERS = 4
CORES = 2
MESH = pl.DeviceIdType.MESH
BF16 = jnp.bfloat16
F32 = jnp.float32
NN = (((1,), (0,)), ((), ()))
NT = (((1,), (1,)), ((), ()))
TN = (((0,), (0,)), ((), ()))


def mm(a, b, dims=NN):
    return lax.dot_general(a, b, dims, preferred_element_type=F32)


def split(a):
    high = a.astype(BF16)
    return high, (a - high.astype(F32)).astype(BF16)


def main_kernel(
    nz, ny, nx, factor,
    grad, slots_in, mom, basis,
    merged_out, ortho_out, right_out, basis_out, o2_out, wall_out,
    momv, recv, merged, turned, perm, slots, current, rs_send, rs_recv, left, grams, w_send, w_recv, wag,
    wall, squares, rightf, ortho, amat, xmat, linv, mom_sem, out_sem, slot_s, slot_r, grad_s, grad_r,
    rs_s, rs_r, sq_s, sq_r, ag_s, ag_r, gram_s, gram_r, wrs_s, wrs_r, wag_s, wag_r, wall_s, wall_r, pair_s, pair_r,
):
    row, col = lax.axis_index("row"), lax.axis_index("col")
    z, y = col // ny, col % ny
    x, core = row // CORES, row % CORES
    n_col, n_row = nz * ny, nx * CORES
    tile_rows, tile_cols = merged.shape
    rank = current.shape[1]
    flat = tile_rows // n_col
    group = flat * ny
    piece = tile_cols // n_row
    quarter = tile_cols // 4
    offsets = [(dz, dy) for dz in range(nz) for dy in range(ny) if (dz, dy) != (0, 0)]
    partner = x * CORES + (1 - core)

    def shifted(dz, dy):
        return lax.rem(z + dz, nz) * ny + lax.rem(y + dy, ny)

    def rows_at(index, size):
        return pl.ds(pl.multiple_of(index * size, size), size)

    def remote(src, dst, send, receive, to_row, to_col):
        return pltpu.make_async_remote_copy(
            src_ref=src, dst_ref=dst, send_sem=send, recv_sem=receive, device_id=(to_row, to_col), device_id_type=MESH
        )

    def await_recv(ref, sem):
        remote(ref, ref, sem, sem, partner, col).wait_recv()

    def await_send(ref, sem):
        remote(ref, ref, sem, sem, partner, col).wait_send()

    load = pltpu.make_async_copy(mom, momv, mom_sem)
    load.start()
    squares[...] = jnp.zeros_like(squares)

    barrier = pltpu.get_barrier_semaphore()
    for dz, dy in offsets:
        pl.semaphore_signal(barrier, inc=1, device_id=(row, shifted(dz, dy)), device_id_type=MESH)
    for d in range(1, n_row):
        pl.semaphore_signal(barrier, inc=1, device_id=(lax.rem(row + d, n_row), col), device_id_type=MESH)
    pl.semaphore_wait(barrier, n_col - 1 + n_row - 1)

    mine = rows_at(col, flat)
    slots[col] = slots_in[...]
    for dz, dy in offsets:
        remote(slots_in, slots.at[col], slot_s, slot_r, row, shifted(dz, dy)).start()

    def columns_of(c):
        return pl.ds(pl.multiple_of(c * tile_cols, 128), tile_cols)

    for dz, dy in offsets:
        to = shifted(dz, dy)
        remote(grad.at[:, columns_of(to)], recv.at[mine, :], grad_s, grad_r.at[col], row, to).start()
    own = pltpu.make_async_copy(grad.at[:, columns_of(col)], recv.at[mine, :], out_sem)
    own.start()

    current[...] = basis[...].astype(BF16)
    await_recv(slots.at[pl.ds(0, n_col - 1)], slot_r)
    await_send(slots.at[pl.ds(0, n_col - 1)], slot_s)

    def fill_perm(c, _):
        named = jnp.broadcast_to(slots[c][0:1, :], (128, 128)).T[:flat] - row * tile_rows
        lane = lax.broadcasted_iota(jnp.int32, (flat, 128), 1)
        for t in range(tile_rows // 128):
            perm[rows_at(c, flat), t * 128 : (t + 1) * 128] = jnp.where(named == lane + t * 128, 1.0, 0.0).astype(BF16)
        return 0

    lax.fori_loop(0, n_col, fill_perm, 0)
    load.wait()

    wide = 256
    n_wide, rest = tile_cols // wide, tile_cols % wide

    def permute_group(g, _):
        block = perm[rows_at(g, group), :]

        def part(t, _):
            cols = rows_at(t, wide)
            merged[rows_at(g, group), cols] = mm(block, momv[:, cols]).astype(BF16)
            return 0

        lax.fori_loop(0, n_wide, part, 0)
        if rest:
            cols = pl.ds(n_wide * wide, rest)
            merged[rows_at(g, group), cols] = mm(block, momv[:, cols]).astype(BF16)
        return 0

    lax.fori_loop(0, nz, permute_group, 0)

    own.wait()
    for dz in range(nz):
        zc = lax.rem(z + dz, nz)
        for dy in range(ny):
            if (dz, dy) != (0, 0):
                c = shifted(dz, dy)
                await_recv(recv.at[rows_at(c, flat), :], grad_r.at[c])

        def add(i, _, zc=zc):
            at = pl.ds(pl.multiple_of(zc * group + i * 32, 32), 32)
            merged[at, :] = (merged[at, :].astype(F32) + recv[at, :].astype(F32)).astype(BF16)
            return 0

        lax.fori_loop(0, group // 32, add, 0)

        def turn(t, _, zc=zc):
            cols = rows_at(t, 128)
            turned[cols, rows_at(zc, group)] = merged[rows_at(zc, group), cols].T
            return 0

        lax.fori_loop(0, tile_cols // 128, turn, 0)
    await_send(recv.at[pl.ds(0, (n_col - 1) * flat), :], grad_s)

    lane = lax.broadcasted_iota(jnp.int32, (8, rank), 1)
    sub = lax.broadcasted_iota(jnp.int32, (8, rank), 0)

    def eliminate(b, _):
        start = b * 8
        at = rows_at(b, 8)
        a, v = amat[at, :], xmat[at, :]
        spread = [
            jnp.broadcast_to(jnp.sum(jnp.where(lane == start + k, a, 0.0), axis=1, keepdims=True), (8, rank))
            for k in range(8)
        ]
        pivots = jnp.ones((8, rank), F32)
        for k in range(8):
            pivot = jnp.broadcast_to(spread[k][k : k + 1, :], (8, rank))
            pivots = jnp.where(sub == k, pivot, pivots)
            if k < 7:
                ratio = jnp.where(sub > k, spread[k] / pivot, 0.0)
                a = a - ratio * jnp.broadcast_to(a[k : k + 1, :], (8, rank))
                v = v - ratio * jnp.broadcast_to(v[k : k + 1, :], (8, rank))
                for j in range(k + 1, 8):
                    spread[j] = spread[j] - ratio * jnp.broadcast_to(spread[j][k : k + 1, :], (8, rank))
        linv[at, :] = v * lax.rsqrt(pivots)
        scaled = jnp.where(lane >= start + 8, a / pivots, 0.0)
        change = lax.dot_general(
            scaled,
            jnp.concatenate([a, v], axis=1),
            TN,
            precision=lax.Precision.HIGHEST,
            preferred_element_type=F32,
        )
        amat[...] -= change[:, :rank]
        xmat[...] -= change[:, rank:]
        return 0

    def iterate(k, _):
        for dz, dy in offsets:
            remote(
                squares.at[col, pl.ds(0, 1)], squares.at[col, pl.ds(0, 1)], sq_s, sq_r, row, shifted(dz, dy)
            ).start()
        for dz in list(range(1, nz)) + [0]:
            zc = lax.rem(z + dz, nz)
            rs_send[rows_at(zc, group), :] = mm(merged[rows_at(zc, group), :], current[...]).astype(BF16)
            for dy in range(ny):
                if (dz, dy) != (0, 0):
                    to = shifted(dz, dy)
                    slot = pl.ds(offsets.index((dz, dy)) * flat, flat)
                    remote(rs_send.at[rows_at(to, flat), :], rs_recv.at[slot, :], rs_s, rs_r, row, to).start()
        await_recv(squares.at[pl.ds(0, n_col - 1), pl.ds(0, 1)], sq_r)
        await_recv(rs_recv, rs_r)
        total = rs_send[mine, :].astype(F32)
        for s in range(n_col - 1):
            total = total + rs_recv[s * flat : (s + 1) * flat, :].astype(F32)
        norm = jnp.sqrt(jnp.sum(squares[:, 0:1, :], axis=0) + 1e-06)
        total = total / jnp.where(k == 0, jnp.ones_like(norm), norm)
        left[mine, :] = total.astype(BF16)
        for dz, dy in offsets:
            remote(left.at[mine, :], left.at[mine, :], ag_s, ag_r, row, shifted(dz, dy)).start()
        await_send(squares.at[pl.ds(0, n_col - 1), pl.ds(0, 1)], sq_s)
        await_send(rs_recv, rs_s)
        xmat[...] = jnp.where(
            lax.broadcasted_iota(jnp.int32, (rank, rank), 0) == lax.broadcasted_iota(jnp.int32, (rank, rank), 1), 1.0, 0.0
        )
        await_recv(rs_recv, ag_r)

        grams[row] = mm(left[...], left[...], TN)
        for d in range(1, n_row):
            remote(grams.at[row], grams.at[row], gram_s, gram_r, lax.rem(row + d, n_row), col).start()
        for dx in list(range(1, nx)) + [0]:
            xc = lax.rem(x + dx, nx)
            w_send[rows_at(xc, CORES * piece), :] = mm(turned[rows_at(xc, CORES * piece), :], left[...]).astype(BF16)
            for dc in range(CORES):
                if (dx, dc) != (0, 0):
                    to = xc * CORES + lax.rem(core + dc, CORES)
                    slot = pl.ds((dx * CORES + dc - 1) * piece, piece)
                    remote(w_send.at[rows_at(to, piece), :], w_recv.at[slot, :], wrs_s, wrs_r, to, col).start()
        await_send(rs_recv, ag_s)
        await_recv(grams.at[pl.ds(0, n_row - 1)], gram_r)
        gram = grams[0]
        for d in range(1, n_row):
            gram = gram + grams[d]
        amat[...] = gram
        lax.fori_loop(0, rank // 16, eliminate, 0)
        await_recv(w_recv, wrs_r)
        here = rows_at(row, piece)
        total = w_send[here, :].astype(F32)
        for s in range(n_row - 1):
            total = total + w_recv[s * piece : (s + 1) * piece, :].astype(F32)
        wag[here, :] = total.astype(BF16)
        for d in range(1, n_row):
            remote(wag.at[here, :], wag.at[here, :], wag_s, wag_r, lax.rem(row + d, n_row), col).start()
        lax.fori_loop(rank // 16, rank // 8, eliminate, 0)
        await_send(grams.at[pl.ds(0, n_row - 1)], gram_s)
        await_send(w_recv, wrs_s)
        await_recv(w_recv, wag_r)
        await_send(w_recv, wag_s)

        high, low = split(linv[...])
        summed = jnp.zeros((1, rank), F32)
        for t in range(4):
            at = slice(t * quarter, (t + 1) * quarter)
            part = mm(wag[at, :], high, NT) + mm(wag[at, :], low, NT)
            rightf[at, :] = part
            current[at, :] = part.astype(BF16)
            summed = summed + jnp.sum(part * part, axis=0, keepdims=True)
        squares[col] = jnp.broadcast_to(summed, (8, rank))
        return 0

    lax.fori_loop(0, ITERS, iterate, 0)

    def cut(c, p):
        return pl.ds(pl.multiple_of(c * tile_cols + (core * 2 + p) * quarter, quarter), quarter)

    def along(p, d):
        return shifted(d, 0) if p == 0 else shifted(0, d)

    def pass_on(p, c):
        for d in range(1, ny):
            to = along(1 - p, d)
            remote(wall.at[cut(c, p), :], wall.at[cut(c, p), :], wall_s, wall_r.at[p, c], row, to).start()

    wall[rows_at(col, tile_cols), :] = wag[...]
    for p in range(2):
        for d in range(1, ny):
            remote(wall.at[cut(col, p), :], wall.at[cut(col, p), :], wall_s, wall_r.at[p, col], row, along(p, d)).start()
    for dz, dy in offsets:
        remote(squares.at[col, pl.ds(0, 1)], squares.at[col, pl.ds(0, 1)], sq_s, sq_r, row, shifted(dz, dy)).start()
    for p in range(2):
        pass_on(p, col)

    def to_partner(p, c):
        remote(wall.at[cut(c, p), :], wall.at[cut(c, p), :], pair_s, pair_r, partner, col).start()

    for d in range(1, ny):
        for p in range(2):
            c = along(p, d)
            await_recv(wall.at[cut(c, p), :], wall_r.at[p, c])
            pass_on(p, c)
            to_partner(p, c)

    high, low = split(linv[...])
    ortho[...] = (mm(left[...], high, NT) + mm(left[...], low, NT)).astype(BF16)
    right_out[...] = current[...]
    await_recv(squares.at[pl.ds(0, n_col - 1), pl.ds(0, 1)], sq_r)
    await_send(squares.at[pl.ds(0, n_col - 1), pl.ds(0, 1)], sq_s)
    norm = jnp.sqrt(jnp.sum(squares[:, 0:1, :], axis=0) + 1e-06)
    basis_out[...] = rightf[...] / norm
    o2 = lax.dot_general(
        ortho[mine, :].astype(F32) * (factor / norm), linv[...], NN, precision=lax.Precision.HIGHEST,
        preferred_element_type=F32,
    )
    high, low = split(o2)
    o2_out[0] = high
    o2_out[1] = low
    ortho_out[...] = mm(perm[...], ortho[...], TN).astype(BF16)

    def restore(t, _):
        at = rows_at(t, wide)
        momv[at, :] = mm(perm[:, at], merged[...], TN).astype(BF16)
        return 0

    lax.fori_loop(0, tile_rows // wide, restore, 0)
    store = pltpu.make_async_copy(momv, merged_out, mom_sem)
    store.start()

    for dz, dy in offsets:
        c = shifted(dz, dy)
        for p in range(2):
            if (dz, dy)[1 - p] != 0:
                await_recv(wall.at[cut(c, p), :], wall_r.at[p, c])
                to_partner(p, c)
    half = (n_col - 1) * 2 * quarter
    await_recv(wall.at[pl.ds(0, half), :], pair_r)
    write = pltpu.make_async_copy(wall, wall_out, out_sem)
    write.start()
    await_send(wall.at[pl.ds(0, half), :], pair_s)
    await_send(wall.at[pl.ds(0, half), :], wall_s)
    store.wait()
    write.wait()


def output_kernel(o2, wall, merged, ortho, right, new_momentum, update):
    w = wall[...]
    update[...] = (mm(o2[0], w, NT) + mm(o2[1], w, NT)).astype(BF16)
    fed_back = mm(ortho[...], right[...], NT)
    new_momentum[...] = (merged[...].astype(F32) - 0.05 * fed_back).astype(BF16)


def shards(nz, ny, nx, flat_grad, flat_rows, momentum, basis):
    tile_rows, tile_cols = momentum.shape
    flat, cols = flat_grad.shape
    rank = basis.shape[1]
    n_col, n_row = nz * ny, nx * CORES
    piece = tile_cols // n_row
    factor = math.sqrt(tile_rows * n_row * cols / rank)
    named = jnp.broadcast_to(jnp.pad(flat_rows, (0, 128 - flat))[None, :], (8, 128))
    dma = pltpu.SemaphoreType.DMA
    any_space = pl.BlockSpec(memory_space=pl.ANY)
    vmem = pl.BlockSpec(memory_space=pltpu.VMEM)
    shape = jax.ShapeDtypeStruct
    merged, ortho, right, new_basis, o2, wall = pl.pallas_call(
        functools.partial(main_kernel, nz, ny, nx, factor),
        out_shape=[
            shape((tile_rows, tile_cols), BF16),
            shape((tile_rows, rank), BF16),
            shape((tile_cols, rank), BF16),
            shape((tile_cols, rank), F32),
            shape((2, flat, rank), BF16),
            shape((cols, rank), BF16),
        ],
        in_specs=[any_space, vmem, any_space, vmem],
        out_specs=[any_space, vmem, vmem, vmem, vmem, any_space],
        scratch_shapes=[
            pltpu.VMEM((tile_rows, tile_cols), BF16),
            pltpu.VMEM((tile_rows, tile_cols), BF16),
            pltpu.VMEM((tile_rows, tile_cols), BF16),
            pltpu.VMEM((tile_cols, tile_rows), BF16),
            pltpu.VMEM((tile_rows, tile_rows), BF16),
            pltpu.VMEM((n_col, 8, 128), jnp.int32),
            pltpu.VMEM((tile_cols, rank), BF16),
            pltpu.VMEM((tile_rows, rank), BF16),
            pltpu.VMEM(((n_col - 1) * flat, rank), BF16),
            pltpu.VMEM((tile_rows, rank), BF16),
            pltpu.VMEM((n_row, rank, rank), F32),
            pltpu.VMEM((tile_cols, rank), BF16),
            pltpu.VMEM(((n_row - 1) * piece, rank), BF16),
            pltpu.VMEM((tile_cols, rank), BF16),
            pltpu.VMEM((cols, rank), BF16),
            pltpu.VMEM((n_col, 8, rank), F32),
            pltpu.VMEM((tile_cols, rank), F32),
            pltpu.VMEM((tile_rows, rank), BF16),
            pltpu.VMEM((rank, rank), F32),
            pltpu.VMEM((rank, rank), F32),
            pltpu.VMEM((rank, rank), F32),
            dma, dma,
            dma, dma,
            dma, dma((n_col,)),
            dma, dma, dma, dma, dma, dma,
            dma, dma, dma, dma, dma, dma,
            dma, dma((2, n_col)),
            dma, dma,
        ],
        compiler_params=pltpu.CompilerParams(
            collective_id=0, has_side_effects=True, vmem_limit_bytes=60 * 1024 * 1024
        ),
        name="dion_main",
    )(flat_grad, named, momentum, basis)

    new_momentum, update = pl.pallas_call(
        output_kernel,
        grid=(n_col,),
        out_shape=[shape((tile_rows, tile_cols), BF16), shape((flat, cols), BF16)],
        in_specs=[
            pl.BlockSpec((2, flat, rank), lambda i: (0, 0, 0)),
            pl.BlockSpec((tile_cols, rank), lambda i: (i, 0)),
            pl.BlockSpec((flat, tile_cols), lambda i: (i, 0)),
            pl.BlockSpec((flat, rank), lambda i: (i, 0)),
            pl.BlockSpec((tile_cols, rank), lambda i: (0, 0)),
        ],
        out_specs=[
            pl.BlockSpec((flat, tile_cols), lambda i: (i, 0)),
            pl.BlockSpec((flat, tile_cols), lambda i: (0, i)),
        ],
        compiler_params=pltpu.CompilerParams(vmem_limit_bytes=40 * 1024 * 1024),
        name="dion_outputs",
    )(o2, wall, merged, ortho, right)
    return new_momentum, new_basis, update


def solution(mesh):
    n_row, n_col = mesh.shape["row"], mesh.shape["col"]
    ny = math.isqrt(n_col)
    return jax.shard_map(
        functools.partial(shards, n_col // ny, ny, n_row // CORES),
        mesh=mesh,
        in_specs=(P(("row", "col"), None), P(("row", "col")), P("row", "col"), P("col", None)),
        out_specs=(P("row", "col"), P("col", None), P(("row", "col"), None)),
        check_vma=False,
    )
```

```python
import functools
import math

import jax
import jax.numpy as jnp
from jax import lax
from jax.experimental import pallas as pl
from jax.experimental.pallas import tpu as pltpu
from jax.sharding import PartitionSpec as P

ITERS = 4
CORES = 2
STEP = 16
ROUND = 32
MESH = pl.DeviceIdType.MESH
BF16 = jnp.bfloat16
F32 = jnp.float32
NN = (((1,), (0,)), ((), ()))
NT = (((1,), (1,)), ((), ()))
TN = (((0,), (0,)), ((), ()))


def mm(a, b, dims=NN):
    return lax.dot_general(a, b, dims, preferred_element_type=F32)


def split(a):
    high = a.astype(BF16)
    return high, (a - high.astype(F32)).astype(BF16)


def main_kernel(
    nz, ny, nx, factor,
    grad, slots_in, mom, basis,
    merged_out, ortho_out, right_out, basis_out, o2_out, wall_out,
    momv, recv, merged, turned, perm, perm_t, slots, current, rs_send, rs_recv, left, gram_own, gram_pair, gram_x, gram_all, w_send, w_pair, w_mid, w_recv, wag,
    wall, squares, rightf, ortho, amat, xmat, linv, mom_sem, out_sem, slot_s, slot_r, grad_s, grad_r,
    rs_s, rs_r, sq_s, sq_r, ag_s, ag_r, gram_s, gram_r, wrs_s, wrs_r, wag_s, wag_r, wall_s, wall_r, pair_s, pair_r,
    half_s, half_r, own_sem, last_s, last_r,
):
    row, col = lax.axis_index("row"), lax.axis_index("col")
    z, y = col // ny, col % ny
    x, core = row // CORES, row % CORES
    n_col, n_row = nz * ny, nx * CORES
    tile_rows, tile_cols = merged.shape
    rank = current.shape[1]
    flat = tile_rows // n_col
    rounds, per_round = flat // ROUND, n_col * ROUND
    group = flat * ny
    piece = tile_cols // n_row
    quarter = tile_cols // 4
    half = tile_cols // CORES
    offsets = [(dz, dy) for dz in range(nz) for dy in range(ny) if (dz, dy) != (0, 0)]
    offsets.sort(key=lambda o: (min(o[0], nz - o[0]) + min(o[1], ny - o[1]), max(o)))
    partner = x * CORES + (1 - core)

    def shifted(dz, dy):
        return lax.rem(z + dz, nz) * ny + lax.rem(y + dy, ny)

    def beside(dx):
        return lax.rem(x + dx, nx) * CORES + core

    def rows_at(index, size):
        return pl.ds(pl.multiple_of(index * size, size), size)

    def remote(src, dst, send, receive, to_row, to_col):
        return pltpu.make_async_remote_copy(
            src_ref=src, dst_ref=dst, send_sem=send, recv_sem=receive, device_id=(to_row, to_col), device_id_type=MESH
        )

    def await_recv(ref, sem):
        remote(ref, ref, sem, sem, partner, col).wait_recv()

    def await_send(ref, sem):
        remote(ref, ref, sem, sem, partner, col).wait_send()

    load = pltpu.make_async_copy(mom, momv, mom_sem)
    load.start()
    squares[...] = jnp.zeros_like(squares)

    barrier = pltpu.get_barrier_semaphore()
    for dz, dy in offsets:
        pl.semaphore_signal(barrier, inc=1, device_id=(row, shifted(dz, dy)), device_id_type=MESH)
    for dx in range(1, nx):
        pl.semaphore_signal(barrier, inc=1, device_id=(beside(dx), col), device_id_type=MESH)
    pl.semaphore_signal(barrier, inc=1, device_id=(partner, col), device_id_type=MESH)
    pl.semaphore_wait(barrier, n_col - 1 + nx)

    mine = rows_at(col, flat)
    slots[col] = jnp.zeros((8, 128), jnp.int32)
    slots[col, 0:1, 0:flat] = slots_in[...]
    for dz, dy in offsets:
        remote(slots.at[col], slots.at[col], slot_s, slot_r, row, shifted(dz, dy)).start()

    def columns_of(c):
        return pl.ds(pl.multiple_of(c * tile_cols, 128), tile_cols)

    def row_of(r, c):
        return pl.ds(pl.multiple_of(r * per_round + c * ROUND, ROUND), ROUND)

    own = []
    for r in range(rounds):
        taken = pl.ds(r * ROUND, ROUND)
        for dz, dy in offsets:
            to = shifted(dz, dy)
            remote(
                grad.at[taken, columns_of(to)], recv.at[row_of(r, col), :], grad_s, grad_r.at[r], row, to
            ).start()
        own.append(
            pltpu.make_async_copy(grad.at[taken, columns_of(col)], recv.at[row_of(r, col), :], own_sem.at[r])
        )
        own[r].start()

    current[...] = basis[...].astype(BF16)
    await_recv(slots.at[pl.ds(0, n_col - 1)], slot_r)
    await_send(slots.at[pl.ds(0, n_col - 1)], slot_s)

    def fill_perm(c, _):
        named = jnp.broadcast_to(slots[c][0:1, :], (128, 128)).T - row * tile_rows
        lanes = lax.broadcasted_iota(jnp.int32, (ROUND, 128), 1)
        for r in range(rounds):
            part = named[r * ROUND : (r + 1) * ROUND]
            for t in range(tile_rows // 128):
                perm[row_of(r, c), t * 128 : (t + 1) * 128] = jnp.where(part == lanes + t * 128, 1.0, 0.0).astype(BF16)
        return 0

    lax.fori_loop(0, n_col, fill_perm, 0)
    load.wait()

    wide = 256
    n_wide, rest = tile_cols // wide, tile_cols % wide

    def permute(target, one, source, at):
        block = one[at, :]

        def part(t, _):
            cols = rows_at(t, wide)
            target[at, cols] = mm(block, source[:, cols]).astype(BF16)
            return 0

        lax.fori_loop(0, n_wide, part, 0)
        if rest:
            cols = pl.ds(n_wide * wide, rest)
            target[at, cols] = mm(block, source[:, cols]).astype(BF16)

    def permute_group(g, _):
        permute(merged, perm, momv, rows_at(g, group))
        return 0

    lax.fori_loop(0, nz, permute_group, 0)

    def turn_perm(t, _):
        cols = rows_at(t, 128)
        perm_t[cols, :] = perm[:, cols].T
        return 0

    lax.fori_loop(0, tile_rows // 128, turn_perm, 0)

    for r in range(rounds):
        begin = r * per_round
        own[r].wait()
        await_recv(recv.at[pl.ds(0, (n_col - 1) * ROUND), :], grad_r.at[r])

        def add(i, _, begin=begin):
            at = pl.ds(pl.multiple_of(begin + i * ROUND, ROUND), ROUND)
            merged[at, :] = (merged[at, :].astype(F32) + recv[at, :].astype(F32)).astype(BF16)
            return 0

        lax.fori_loop(0, n_col, add, 0)

        def turn(t, _, begin=begin):
            cols = rows_at(t, 128)
            turned[cols, begin : begin + per_round] = merged[begin : begin + per_round, cols].T
            return 0

        lax.fori_loop(0, tile_cols // 128, turn, 0)
    await_send(recv.at[pl.ds(0, (n_col - 1) * flat), :], grad_s)

    lane = lax.broadcasted_iota(jnp.int32, (STEP, rank), 1)
    sub = lax.broadcasted_iota(jnp.int32, (STEP, rank), 0)

    def eliminate(b, _):
        start = b * STEP
        at = rows_at(b, STEP)
        a, v = amat[at, :], xmat[at, :]
        spread = [
            jnp.broadcast_to(jnp.sum(jnp.where(lane == start + k, a, 0.0), axis=1, keepdims=True), (STEP, rank))
            for k in range(STEP)
        ]
        inverse = jnp.ones((STEP, rank), F32)
        for k in range(STEP):
            one_over = 1.0 / jnp.broadcast_to(spread[k][k : k + 1, :], (STEP, rank))
            inverse = jnp.where(sub == k, one_over, inverse)
            if k < STEP - 1:
                ratio = jnp.where(sub > k, spread[k] * one_over, 0.0)
                a = a - ratio * jnp.broadcast_to(a[k : k + 1, :], (STEP, rank))
                v = v - ratio * jnp.broadcast_to(v[k : k + 1, :], (STEP, rank))
                for j in range(k + 1, STEP):
                    spread[j] = spread[j] - ratio * jnp.broadcast_to(spread[j][k : k + 1, :], (STEP, rank))
        linv[at, :] = v * jnp.sqrt(inverse)
        scaled = jnp.where(lane >= start + STEP, a * inverse, 0.0)
        change = lax.dot_general(
            scaled,
            jnp.concatenate([a, v], axis=1),
            TN,
            precision=lax.Precision.HIGHEST,
            preferred_element_type=F32,
        )
        amat[...] -= change[:, :rank]
        xmat[...] -= change[:, rank:]
        return 0

    steps = rank // STEP
    gram_half = rank // CORES
    core_rows = rows_at(core, half)
    other_rows = rows_at(1 - core, half)

    def iterate(k, _):
        for dz in list(range(1, nz)) + [0]:
            zc = lax.rem(z + dz, nz)
            rs_send[rows_at(zc, group), :] = mm(merged[rows_at(zc, group), :], current[...]).astype(BF16)
            for dy in range(ny):
                if (dz, dy) != (0, 0):
                    to = shifted(dz, dy)
                    slot = pl.ds(offsets.index((dz, dy)) * flat, flat)
                    remote(rs_send.at[rows_at(to, flat), :], rs_recv.at[slot, :], rs_s, rs_r, row, to).start()
        for dz, dy in offsets:
            remote(
                squares.at[col, pl.ds(0, 1)], squares.at[col, pl.ds(0, 1)], sq_s, sq_r, row, shifted(dz, dy)
            ).start()
        await_recv(squares.at[pl.ds(0, n_col - 1), pl.ds(0, 1)], sq_r)
        await_recv(rs_recv, rs_r)
        total = rs_send[mine, :].astype(F32)
        for s in range(n_col - 1):
            total = total + rs_recv[s * flat : (s + 1) * flat, :].astype(F32)
        norm = jnp.sqrt(jnp.sum(squares[:, 0:1, :], axis=0) + 1e-06)
        total = total / jnp.where(k == 0, jnp.ones_like(norm), norm)
        left[mine, :] = total.astype(BF16)
        for dz, dy in offsets:
            remote(left.at[mine, :], left.at[mine, :], ag_s, ag_r, row, shifted(dz, dy)).start()
        await_send(squares.at[pl.ds(0, n_col - 1), pl.ds(0, 1)], sq_s)
        await_send(rs_recv, rs_s)
        xmat[...] = jnp.where(
            lax.broadcasted_iota(jnp.int32, (rank, rank), 0) == lax.broadcasted_iota(jnp.int32, (rank, rank), 1), 1.0, 0.0
        )
        permute(momv, perm_t, merged, rows_at(k, tile_rows // ITERS))
        await_recv(rs_recv, ag_r)

        gram_own[...] = mm(left[...], left[...], TN)
        to_pair = remote(gram_own, gram_pair, gram_s, gram_r, partner, col)
        to_pair.start()
        w_send[...] = mm(turned[other_rows, :], left[...]).astype(BF16)
        w_to_pair = remote(w_send, w_pair, wrs_s.at[0], wrs_r.at[0], partner, col)
        w_to_pair.start()
        await_recv(gram_pair, gram_r)
        gram_rows = rows_at(core, gram_half)
        gram_x[x] = gram_own[gram_rows, :] + gram_pair[gram_rows, :]
        for dx in range(1, nx):
            remote(gram_x.at[x], gram_x.at[x], half_s.at[0], half_r.at[0], beside(dx), col).start()
        own_half = mm(turned[core_rows, :], left[...])
        await_recv(w_pair, wrs_r.at[0])
        w_mid[...] = (own_half + w_pair[...].astype(F32)).astype(BF16)
        for dx in range(1, nx):
            to = lax.rem(x + dx, nx)
            slot = pl.ds((dx - 1) * piece, piece)
            remote(w_mid.at[rows_at(to, piece), :], w_recv.at[slot, :], wrs_s.at[1], wrs_r.at[1], beside(dx), col).start()
        await_send(rs_recv, ag_s)
        await_recv(gram_x.at[pl.ds(0, nx - 1)], half_r.at[0])
        gram = gram_x[0]
        for d in range(1, nx):
            gram = gram + gram_x[d]
        gram_all[gram_rows, :] = gram
        halves = remote(gram_all.at[gram_rows, :], gram_all.at[gram_rows, :], half_s.at[1], half_r.at[1], partner, col)
        halves.start()
        await_recv(gram_all.at[gram_rows, :], half_r.at[1])
        amat[...] = gram_all[...]
        lax.fori_loop(0, 2, eliminate, 0)
        await_recv(w_recv, wrs_r.at[1])
        total = w_mid[rows_at(x, piece), :].astype(F32)
        for d in range(nx - 1):
            total = total + w_recv[d * piece : (d + 1) * piece, :].astype(F32)

        def held(xc):
            return rows_at(core * nx + xc, piece)

        wag[held(x), :] = total.astype(BF16)
        for dx in range(1, nx):
            remote(wag.at[held(x), :], wag.at[held(x), :], wag_s, wag_r.at[x], beside(dx), col).start()
        remote(wag.at[held(x), :], wag.at[held(x), :], pair_s, pair_r, partner, col).start()
        lax.fori_loop(2, steps, eliminate, 0)
        for dx in range(1, nx):
            xc = lax.rem(x + dx, nx)
            await_recv(wag.at[held(xc), :], wag_r.at[xc])
            remote(wag.at[held(xc), :], wag.at[held(xc), :], pair_s, pair_r, partner, col).start()
        to_pair.wait_send()
        w_to_pair.wait_send()
        await_send(gram_x.at[pl.ds(0, nx - 1)], half_s.at[0])
        halves.wait_send()
        await_send(w_recv, wrs_s.at[1])
        await_send(w_recv, wag_s)
        await_recv(w_pair, pair_r)
        await_send(w_pair, pair_s)

        high, low = split(linv[...])
        summed = jnp.zeros((1, rank), F32)
        for t in range(4):
            at = slice(t * quarter, (t + 1) * quarter)
            part = mm(wag[at, :], high, NT) + mm(wag[at, :], low, NT)
            rightf[at, :] = part
            current[at, :] = part.astype(BF16)
            summed = summed + jnp.sum(part * part, axis=0, keepdims=True)
        squares[col] = jnp.broadcast_to(summed, (8, rank))
        return 0

    lax.fori_loop(0, ITERS, iterate, 0)

    store = pltpu.make_async_copy(momv, merged_out, mom_sem)
    store.start()

    def cut(c, p):
        return pl.ds(pl.multiple_of(c * tile_cols + (core * 2 + p) * quarter, quarter), quarter)

    def cut_half(c, p, h):
        part = quarter // 2
        return pl.ds(pl.multiple_of(c * tile_cols + (core * 2 + p) * quarter + h * part, part), part)

    def along(p, a, b):
        return shifted(a, b) if p == 0 else shifted(b, a)

    def send_part(at, p, c, to):
        remote(wall.at[at, :], wall.at[at, :], wall_s, wall_r.at[p, c], row, to).start()

    def to_partner(p, c):
        remote(wall.at[cut(c, p), :], wall.at[cut(c, p), :], last_s, last_r, partner, col).start()

    near = (1, ny - 1) if ny == 4 else tuple(range(1, ny))
    far = (2,) if ny == 4 else ()

    def pass_near(p, c, axis, d):
        if far:
            to = along(p, ny - d, 0) if axis == 0 else along(p, 0, ny - d)
            send_part(cut_half(c, p, 0 if d == 1 else 1), p, c, to)

    def spread_second(p, c):
        for d in near:
            send_part(cut(c, p), p, c, along(p, 0, d))

    def arrived(p, a, b):
        c = along(p, a, b)
        await_recv(wall.at[cut(c, p), :], wall_r.at[p, c])
        return c

    wall[rows_at(col, tile_cols), :] = current[...]
    for p in range(2):
        for d in near:
            send_part(cut(col, p), p, col, along(p, d, 0))
    for p in range(2):
        spread_second(p, col)
    for dz, dy in offsets:
        remote(squares.at[col, pl.ds(0, 1)], squares.at[col, pl.ds(0, 1)], sq_s, sq_r, row, shifted(dz, dy)).start()
    high, low = split(linv[...])
    ortho[...] = (mm(left[...], high, NT) + mm(left[...], low, NT)).astype(BF16)
    right_out[...] = current[...]
    for a in near:
        for p in range(2):
            c = arrived(p, a, 0)
            pass_near(p, c, 0, a)
            spread_second(p, c)
            to_partner(p, c)
    for b in near:
        for p in range(2):
            c = arrived(p, 0, b)
            pass_near(p, c, 1, b)
            to_partner(p, c)
    for a in far:
        for p in range(2):
            c = arrived(p, a, 0)
            spread_second(p, c)
            to_partner(p, c)
    await_recv(squares.at[pl.ds(0, n_col - 1), pl.ds(0, 1)], sq_r)
    await_send(squares.at[pl.ds(0, n_col - 1), pl.ds(0, 1)], sq_s)
    norm = jnp.sqrt(jnp.sum(squares[:, 0:1, :], axis=0) + 1e-06)
    basis_out[...] = rightf[...] / norm
    for r in range(rounds):
        o2_out[r * ROUND : (r + 1) * ROUND, :] = (ortho[row_of(r, col), :].astype(F32) * (factor / norm)).astype(BF16)
    for a in near:
        for b in near:
            for p in range(2):
                c = arrived(p, a, b)
                pass_near(p, c, 1, b)
                to_partner(p, c)
    ortho_out[...] = mm(perm_t[...], ortho[...]).astype(BF16)
    for b in far:
        for p in range(2):
            to_partner(p, arrived(p, 0, b))
    for a in far:
        for b in near:
            for p in range(2):
                c = arrived(p, a, b)
                pass_near(p, c, 1, b)
                to_partner(p, c)
    for a in near + far:
        for b in far:
            for p in range(2):
                to_partner(p, arrived(p, a, b))
    most = (n_col - 1) * 2 * quarter
    await_recv(wall.at[pl.ds(0, most), :], last_r)
    write = pltpu.make_async_copy(wall, wall_out, out_sem)
    write.start()
    await_send(wall.at[pl.ds(0, most), :], last_s)
    await_send(wall.at[pl.ds(0, most), :], wall_s)
    store.wait()
    write.wait()


def output_kernel(
    parts, o2, ortho, right, wall, merged, basis, new_momentum, update, new_basis,
    wall_v, merged_v, basis_v, update_v, in_sem, out_sem,
):
    flat, cols = update.shape
    tile_rows = merged.shape[0]
    some_rows, some_cols = tile_rows // parts, cols // parts
    loads, stores = [], [pltpu.make_async_copy(basis_v, new_basis, out_sem.at[2, 0])]
    for i in range(parts):
        at, of = pl.ds(i * some_rows, some_rows), pl.ds(i * some_cols, some_cols)
        loads.append(pltpu.make_async_copy(wall.at[of, :], wall_v.at[of, :], in_sem.at[0, i]))
        loads.append(pltpu.make_async_copy(merged.at[at, :], merged_v.at[at, :], in_sem.at[1, i]))
        stores.append(pltpu.make_async_copy(update_v.at[:, of], update.at[:, of], out_sem.at[0, i]))
        stores.append(pltpu.make_async_copy(merged_v.at[at, :], new_momentum.at[at, :], out_sem.at[1, i]))
    loads.append(pltpu.make_async_copy(basis, basis_v, in_sem.at[2, 0]))
    for load in loads:
        load.start()
    for i in range(parts):
        at, of = pl.ds(i * some_rows, some_rows), pl.ds(i * some_cols, some_cols)
        loads[2 * i].wait()
        update_v[:, of] = mm(o2[...], wall_v[of, :], NT).astype(BF16)
        stores[2 * i + 1].start()
        loads[2 * i + 1].wait()
        fed_back = mm(ortho[at, :], right[...], NT)
        merged_v[at, :] = (merged_v[at, :].astype(F32) - 0.05 * fed_back).astype(BF16)
        stores[2 * i + 2].start()
    loads[2 * parts].wait()
    stores[0].start()
    for store in stores:
        store.wait()


def shards(nz, ny, nx, flat_grad, flat_rows, momentum, basis):
    tile_rows, tile_cols = momentum.shape
    flat, cols = flat_grad.shape
    rank = basis.shape[1]
    n_col, n_row = nz * ny, nx * CORES
    piece = tile_cols // n_row
    half = tile_cols // CORES
    factor = math.sqrt(tile_rows * n_row * cols / rank)
    dma = pltpu.SemaphoreType.DMA
    any_space = pl.BlockSpec(memory_space=pl.ANY)
    vmem = pl.BlockSpec(memory_space=pltpu.VMEM)
    shape = jax.ShapeDtypeStruct
    merged, ortho, right, new_basis, o2, wall = pl.pallas_call(
        functools.partial(main_kernel, nz, ny, nx, factor),
        out_shape=[
            shape((tile_rows, tile_cols), BF16),
            shape((tile_rows, rank), BF16),
            shape((tile_cols, rank), BF16),
            shape((tile_cols, rank), F32),
            shape((flat, rank), BF16),
            shape((cols, rank), BF16),
        ],
        in_specs=[any_space, vmem, any_space, vmem],
        out_specs=[any_space, vmem, vmem, vmem, vmem, any_space],
        scratch_shapes=[
            pltpu.VMEM((tile_rows, tile_cols), BF16),
            pltpu.VMEM((tile_rows, tile_cols), BF16),
            pltpu.VMEM((tile_rows, tile_cols), BF16),
            pltpu.VMEM((tile_cols, tile_rows), BF16),
            pltpu.VMEM((tile_rows, tile_rows), BF16),
            pltpu.VMEM((tile_rows, tile_rows), BF16),
            pltpu.VMEM((n_col, 8, 128), jnp.int32),
            pltpu.VMEM((tile_cols, rank), BF16),
            pltpu.VMEM((tile_rows, rank), BF16),
            pltpu.VMEM(((n_col - 1) * flat, rank), BF16),
            pltpu.VMEM((tile_rows, rank), BF16),
            pltpu.VMEM((rank, rank), F32),
            pltpu.VMEM((rank, rank), F32),
            pltpu.VMEM((nx, rank // CORES, rank), F32),
            pltpu.VMEM((rank, rank), F32),
            pltpu.VMEM((half, rank), BF16),
            pltpu.VMEM((half, rank), BF16),
            pltpu.VMEM((half, rank), BF16),
            pltpu.VMEM(((nx - 1) * piece, rank), BF16),
            pltpu.VMEM((tile_cols, rank), BF16),
            pltpu.VMEM((cols, rank), BF16),
            pltpu.VMEM((n_col, 8, rank), F32),
            pltpu.VMEM((tile_cols, rank), F32),
            pltpu.VMEM((tile_rows, rank), BF16),
            pltpu.VMEM((rank, rank), F32),
            pltpu.VMEM((rank, rank), F32),
            pltpu.VMEM((rank, rank), F32),
            dma, dma,
            dma, dma,
            dma, dma((flat // ROUND,)),
            dma, dma, dma, dma, dma, dma,
            dma, dma, dma((2,)), dma((2,)), dma, dma((nx,)),
            dma, dma((2, n_col)),
            dma, dma,
            dma((2,)), dma((2,)),
            dma((flat // ROUND,)),
            dma, dma,
        ],
        compiler_params=pltpu.CompilerParams(
            collective_id=0, has_side_effects=True, vmem_limit_bytes=60 * 1024 * 1024
        ),
        name="dion_main",
    )(flat_grad, flat_rows.reshape(1, flat), momentum, basis)

    parts = 8
    new_momentum, update, new_basis = pl.pallas_call(
        functools.partial(output_kernel, parts),
        out_shape=[
            shape((tile_rows, tile_cols), BF16),
            shape((flat, cols), BF16),
            shape((tile_cols, rank), F32),
        ],
        in_specs=[vmem, vmem, vmem, any_space, any_space, any_space],
        out_specs=[any_space, any_space, any_space],
        scratch_shapes=[
            pltpu.VMEM((cols, rank), BF16),
            pltpu.VMEM((tile_rows, tile_cols), BF16),
            pltpu.VMEM((tile_cols, rank), F32),
            pltpu.VMEM((flat, cols), BF16),
            dma((3, parts)),
            dma((3, parts)),
        ],
        compiler_params=pltpu.CompilerParams(vmem_limit_bytes=60 * 1024 * 1024),
        name="dion_outputs",
    )(o2, ortho, right, wall, merged, new_basis)
    return new_momentum, new_basis, update


def solution(mesh):
    n_row, n_col = mesh.shape["row"], mesh.shape["col"]
    ny = math.isqrt(n_col)
    return jax.shard_map(
        functools.partial(shards, n_col // ny, ny, n_row // CORES),
        mesh=mesh,
        in_specs=(P(("row", "col"), None), P(("row", "col")), P("row", "col"), P("col", None)),
        out_specs=(P("row", "col"), P("col", None), P(("row", "col"), None)),
        check_vma=False,
    )
```

```python
import functools
import math

import jax
import jax.numpy as jnp
from jax import lax
from jax.experimental import pallas as pl
from jax.experimental.pallas import tpu as pltpu
from jax.sharding import PartitionSpec as P

ITERS = 4
CORES = 2
STEP = 16
ROUND = 32
CHUNKS = 2
MESH = pl.DeviceIdType.MESH
BF16 = jnp.bfloat16
F32 = jnp.float32
NN = (((1,), (0,)), ((), ()))
NT = (((1,), (1,)), ((), ()))
TN = (((0,), (0,)), ((), ()))


def mm(a, b, dims=NN):
    return lax.dot_general(a, b, dims, preferred_element_type=F32)


def split(a):
    high = a.astype(BF16)
    return high, (a - high.astype(F32)).astype(BF16)


def main_kernel(
    nz, ny, nx, factor,
    grad, slots_in, mom, basis,
    merged_out, ortho_out, right_out, basis_out, o2_out, wall,
    momv, recv, merged, turned, perm, perm_t, named_in, slots, current, rs_send, rs_recv, left, gram_own, gram_pair, gram_x, gram_all, w_send, w_pair, w_mid, w_recv, wag,
    w_sum, squares, rightf, ortho, amat, xmat, linv, mom_sem, out_sem, slot_s, slot_r, grad_s, grad_r,
    rs_s, rs_r, sq_s, sq_r, ag_s, ag_r, gram_s, gram_r, wrs_s, wrs_r, wag_s, wag_r, wall_s, wall_r, pair_s, pair_r,
    half_s, half_r, own_sem, last_s, last_r,
):
    row, col = lax.axis_index("row"), lax.axis_index("col")
    z, y = col // ny, col % ny
    x, core = row // CORES, row % CORES
    n_col, n_row = nz * ny, nx * CORES
    tile_rows, tile_cols = merged.shape
    rank = current.shape[1]
    flat = tile_rows // n_col
    rounds, per_round = flat // ROUND, n_col * ROUND
    group = flat * ny
    piece = tile_cols // n_row
    quarter = tile_cols // 4
    half = tile_cols // CORES
    offsets = [(dz, dy) for dz in range(nz) for dy in range(ny) if (dz, dy) != (0, 0)]
    offsets.sort(key=lambda o: (min(o[0], nz - o[0]) + min(o[1], ny - o[1]), max(o)))
    far_first = offsets[::-1]
    across = sorted(range(1, nx), key=lambda d: -min(d, nx - d))
    partner = x * CORES + (1 - core)

    def shifted(dz, dy):
        return lax.rem(z + dz, nz) * ny + lax.rem(y + dy, ny)

    def beside(dx):
        return lax.rem(x + dx, nx) * CORES + core

    def rows_at(index, size):
        return pl.ds(pl.multiple_of(index * size, size), size)

    def remote(src, dst, send, receive, to_row, to_col):
        return pltpu.make_async_remote_copy(
            src_ref=src, dst_ref=dst, send_sem=send, recv_sem=receive, device_id=(to_row, to_col), device_id_type=MESH
        )

    def await_recv(ref, sem):
        remote(ref, ref, sem, sem, partner, col).wait_recv()

    def await_send(ref, sem):
        remote(ref, ref, sem, sem, partner, col).wait_send()

    load = pltpu.make_async_copy(mom, momv, mom_sem)
    load.start()
    load_basis = pltpu.make_async_copy(basis, rightf, half_s.at[0])
    load_basis.start()
    load_slots = pltpu.make_async_copy(slots_in, named_in, half_s.at[1])
    load_slots.start()
    squares[...] = jnp.zeros_like(squares)

    barrier = pltpu.get_barrier_semaphore()
    for dz, dy in offsets:
        pl.semaphore_signal(barrier, inc=1, device_id=(row, shifted(dz, dy)), device_id_type=MESH)
    for dx in range(1, nx):
        pl.semaphore_signal(barrier, inc=1, device_id=(beside(dx), col), device_id_type=MESH)
    pl.semaphore_signal(barrier, inc=1, device_id=(partner, col), device_id_type=MESH)
    pl.semaphore_wait(barrier, n_col - 1 + nx)

    slots[col] = jnp.zeros((8, 128), jnp.int32)
    load_slots.wait()
    slots[col, 0:1, 0:flat] = named_in[...]
    for dz, dy in offsets:
        remote(slots.at[col], slots.at[col], slot_s, slot_r, row, shifted(dz, dy)).start()

    def columns_of(c):
        return pl.ds(pl.multiple_of(c * tile_cols, 128), tile_cols)

    def row_of(r, c):
        return pl.ds(pl.multiple_of(r * per_round + c * ROUND, ROUND), ROUND)

    own = []
    for r in range(rounds):
        taken = pl.ds(r * ROUND, ROUND)
        for dz, dy in offsets:
            to = shifted(dz, dy)
            remote(
                grad.at[taken, columns_of(to)], recv.at[row_of(r, col), :], grad_s, grad_r.at[r], row, to
            ).start()
        own.append(
            pltpu.make_async_copy(grad.at[taken, columns_of(col)], recv.at[row_of(r, col), :], own_sem.at[r])
        )
        own[r].start()

    load_basis.wait()
    current[...] = rightf[...].astype(BF16)
    await_recv(slots.at[pl.ds(0, n_col - 1)], slot_r)
    await_send(slots.at[pl.ds(0, n_col - 1)], slot_s)

    def fill_perm(c, _):
        named = jnp.broadcast_to(slots[c][0:1, :], (128, 128)).T - row * tile_rows
        lanes = lax.broadcasted_iota(jnp.int32, (ROUND, 128), 1)
        for r in range(rounds):
            part = named[r * ROUND : (r + 1) * ROUND]
            for t in range(tile_rows // 128):
                perm[row_of(r, c), t * 128 : (t + 1) * 128] = jnp.where(part == lanes + t * 128, 1.0, 0.0).astype(BF16)
        return 0

    lax.fori_loop(0, n_col, fill_perm, 0)
    load.wait()

    wide = 256
    n_wide, rest = tile_cols // wide, tile_cols % wide

    def permute(target, one, source, at):
        block = one[at, :]

        def part(t, _):
            cols = rows_at(t, wide)
            target[at, cols] = mm(block, source[:, cols]).astype(BF16)
            return 0

        lax.fori_loop(0, n_wide, part, 0)
        if rest:
            cols = pl.ds(n_wide * wide, rest)
            target[at, cols] = mm(block, source[:, cols]).astype(BF16)

    def permute_group(g, _):
        permute(merged, perm, momv, rows_at(g, group))
        return 0

    lax.fori_loop(0, nz, permute_group, 0)

    def turn_perm(t, _):
        cols = rows_at(t, 128)
        perm_t[cols, :] = perm[:, cols].T
        return 0

    lax.fori_loop(0, tile_rows // 128, turn_perm, 0)

    for r in range(rounds):
        begin = r * per_round
        own[r].wait()
        await_recv(recv.at[pl.ds(0, (n_col - 1) * ROUND), :], grad_r.at[r])

        def add(i, _, begin=begin):
            at = pl.ds(pl.multiple_of(begin + i * ROUND, ROUND), ROUND)
            merged[at, :] = (merged[at, :].astype(F32) + recv[at, :].astype(F32)).astype(BF16)
            return 0

        lax.fori_loop(0, n_col, add, 0)

        def turn(t, _, begin=begin):
            cols = rows_at(t, 128)
            turned[cols, begin : begin + per_round] = merged[begin : begin + per_round, cols].T
            return 0

        lax.fori_loop(0, tile_cols // 128, turn, 0)
    await_send(recv.at[pl.ds(0, (n_col - 1) * flat), :], grad_s)

    lane = lax.broadcasted_iota(jnp.int32, (STEP, rank), 1)
    sub = lax.broadcasted_iota(jnp.int32, (STEP, rank), 0)

    def eliminate(b, _):
        start = b * STEP
        at = rows_at(b, STEP)
        a, v = amat[at, :], xmat[at, :]
        spread = [
            jnp.broadcast_to(jnp.sum(jnp.where(lane == start + k, a, 0.0), axis=1, keepdims=True), (STEP, rank))
            for k in range(STEP)
        ]
        inverse = jnp.ones((STEP, rank), F32)
        for k in range(STEP):
            one_over = 1.0 / jnp.broadcast_to(spread[k][k : k + 1, :], (STEP, rank))
            inverse = jnp.where(sub == k, one_over, inverse)
            if k < STEP - 1:
                ratio = jnp.where(sub > k, spread[k] * one_over, 0.0)
                a = a - ratio * jnp.broadcast_to(a[k : k + 1, :], (STEP, rank))
                v = v - ratio * jnp.broadcast_to(v[k : k + 1, :], (STEP, rank))
                for j in range(k + 1, STEP):
                    spread[j] = spread[j] - ratio * jnp.broadcast_to(spread[j][k : k + 1, :], (STEP, rank))
        linv[at, :] = v * jnp.sqrt(inverse)
        scaled = jnp.where(lane >= start + STEP, a * inverse, 0.0)
        change = lax.dot_general(
            scaled,
            jnp.concatenate([a, v], axis=1),
            TN,
            precision=lax.Precision.HIGHEST,
            preferred_element_type=F32,
        )
        amat[...] -= change[:, :rank]
        xmat[...] -= change[:, rank:]
        return 0

    steps = rank // STEP
    chunk, share = tile_rows // CHUNKS, flat // CHUNKS
    restored = tile_rows // (2 * ITERS)

    def share_of(h, c):
        return pl.ds(pl.multiple_of(h * chunk + c * share, share), share)

    def others(ref, h):
        return ref.at[pl.ds(h * (n_col - 1) * share, (n_col - 1) * share), :]

    gram_half = rank // CORES
    core_rows = rows_at(core, half)
    other_rows = rows_at(1 - core, half)

    def iterate(k, _):
        for h in range(CHUNKS):
            at = slice(h * chunk, (h + 1) * chunk)
            rs_send[at, :] = mm(merged[at, :], current[...]).astype(BF16)
            for i, (dz, dy) in enumerate(far_first):
                to = shifted(dz, dy)
                slot = pl.ds((h * (n_col - 1) + i) * share, share)
                remote(rs_send.at[share_of(h, to), :], rs_recv.at[slot, :], rs_s.at[h], rs_r.at[h], row, to).start()
            if h == 0:
                for dz, dy in offsets:
                    to = shifted(dz, dy)
                    remote(squares.at[col, pl.ds(0, 1)], squares.at[col, pl.ds(0, 1)], sq_s, sq_r, row, to).start()
        permute(momv, perm_t, merged, rows_at(2 * k, restored))
        await_recv(squares.at[pl.ds(0, n_col - 1), pl.ds(0, 1)], sq_r)
        norm = jnp.sqrt(jnp.sum(squares[:, 0:1, :], axis=0) + 1e-06)
        scale = 1.0 / jnp.where(k == 0, jnp.ones_like(norm), norm)
        for h in range(CHUNKS):
            await_recv(others(rs_recv, h), rs_r.at[h])
            total = rs_send[share_of(h, col), :].astype(F32)
            for i in range(n_col - 1):
                begin = (h * (n_col - 1) + i) * share
                total = total + rs_recv[begin : begin + share, :].astype(F32)
            left[share_of(h, col), :] = (total * scale).astype(BF16)
            for dz, dy in far_first:
                ours = left.at[share_of(h, col), :]
                remote(ours, ours, ag_s.at[h], ag_r.at[h], row, shifted(dz, dy)).start()
        xmat[...] = jnp.where(
            lax.broadcasted_iota(jnp.int32, (rank, rank), 0) == lax.broadcasted_iota(jnp.int32, (rank, rank), 1), 1.0, 0.0
        )
        await_send(squares.at[pl.ds(0, n_col - 1), pl.ds(0, 1)], sq_s)
        for h in range(CHUNKS):
            await_send(others(rs_recv, h), rs_s.at[h])

        first, second = slice(0, chunk), slice(chunk, 2 * chunk)
        await_recv(others(rs_recv, 0), ag_r.at[0])
        w_sum[...] = mm(turned[:, first], left[first, :])
        gram_own[...] = mm(left[first, :], left[first, :], TN)
        await_recv(others(rs_recv, 1), ag_r.at[1])
        gram_own[...] += mm(left[second, :], left[second, :], TN)
        to_pair = remote(gram_own, gram_pair, gram_s, gram_r, partner, col)
        to_pair.start()
        w_send[...] = (w_sum[other_rows, :] + mm(turned[other_rows, second], left[second, :])).astype(BF16)
        w_to_pair = remote(w_send, w_pair, wrs_s.at[0], wrs_r.at[0], partner, col)
        w_to_pair.start()
        await_recv(gram_pair, gram_r)
        gram_rows = rows_at(core, gram_half)
        gram_x[x] = gram_own[gram_rows, :] + gram_pair[gram_rows, :]
        for dx in across:
            remote(gram_x.at[x], gram_x.at[x], half_s.at[0], half_r.at[0], beside(dx), col).start()
        own_half = w_sum[core_rows, :] + mm(turned[core_rows, second], left[second, :])
        await_recv(w_pair, wrs_r.at[0])
        w_mid[...] = (own_half + w_pair[...].astype(F32)).astype(BF16)
        for dx in across:
            to = lax.rem(x + dx, nx)
            slot = pl.ds((dx - 1) * piece, piece)
            remote(w_mid.at[rows_at(to, piece), :], w_recv.at[slot, :], wrs_s.at[1], wrs_r.at[1], beside(dx), col).start()
        for h in range(CHUNKS):
            await_send(others(rs_recv, h), ag_s.at[h])
        permute(momv, perm_t, merged, rows_at(2 * k + 1, restored))
        await_recv(gram_x.at[pl.ds(0, nx - 1)], half_r.at[0])
        gram = gram_x[0]
        for d in range(1, nx):
            gram = gram + gram_x[d]
        gram_all[gram_rows, :] = gram
        halves = remote(gram_all.at[gram_rows, :], gram_all.at[gram_rows, :], half_s.at[1], half_r.at[1], partner, col)
        halves.start()
        await_recv(gram_all.at[gram_rows, :], half_r.at[1])
        amat[...] = gram_all[...]
        lax.fori_loop(0, 1, eliminate, 0)
        await_recv(w_recv, wrs_r.at[1])
        total = w_mid[rows_at(x, piece), :].astype(F32)
        for d in range(nx - 1):
            total = total + w_recv[d * piece : (d + 1) * piece, :].astype(F32)

        def held(xc):
            return rows_at(core * nx + xc, piece)

        wag[held(x), :] = total.astype(BF16)
        for dx in across:
            remote(wag.at[held(x), :], wag.at[held(x), :], wag_s, wag_r.at[x], beside(dx), col).start()
        remote(wag.at[held(x), :], wag.at[held(x), :], pair_s, pair_r, partner, col).start()
        lax.fori_loop(1, steps - 1, eliminate, 0)
        for dx in range(1, nx):
            xc = lax.rem(x + dx, nx)
            await_recv(wag.at[held(xc), :], wag_r.at[xc])
            remote(wag.at[held(xc), :], wag.at[held(xc), :], pair_s, pair_r, partner, col).start()
        lax.fori_loop(steps - 1, steps, eliminate, 0)
        to_pair.wait_send()
        w_to_pair.wait_send()
        await_send(gram_x.at[pl.ds(0, nx - 1)], half_s.at[0])
        halves.wait_send()
        await_send(w_recv, wrs_s.at[1])
        await_send(w_recv, wag_s)
        await_recv(w_pair, pair_r)
        await_send(w_pair, pair_s)

        high, low = split(linv[...])
        summed = jnp.zeros((1, rank), F32)
        for t in range(4):
            at = slice(t * quarter, (t + 1) * quarter)
            part = mm(wag[at, :], high, NT) + mm(wag[at, :], low, NT)
            rightf[at, :] = part
            current[at, :] = part.astype(BF16)
            summed = summed + jnp.sum(part * part, axis=0, keepdims=True)
        squares[col] = jnp.broadcast_to(summed, (8, rank))
        return 0

    lax.fori_loop(0, ITERS, iterate, 0)

    store = pltpu.make_async_copy(momv, merged_out, mom_sem)
    store.start()

    def turn_right(t, _):
        at = rows_at(t, 128)
        right_out[:, at] = current[at, :].T
        return 0

    lax.fori_loop(0, tile_cols // 128, turn_right, 0)

    rank_part = rank // 4

    def cut(c, p):
        return pl.ds(pl.multiple_of((core * 2 + p) * rank_part, rank_part), rank_part), columns_of(c)

    def cut_half(c, p, h):
        size = rank_part // 2
        return pl.ds(pl.multiple_of((core * 2 + p) * rank_part + h * size, size), size), columns_of(c)

    def along(p, a, b):
        return shifted(a, b) if p == 0 else shifted(b, a)

    def send_own(p, to):
        part, cols = cut(col, p)
        remote(right_out.at[part, :], wall.at[part, cols], wall_s, wall_r.at[p, col], row, to).start()

    def send_part(at, p, c, to):
        remote(wall.at[at], wall.at[at], wall_s, wall_r.at[p, c], row, to).start()

    def to_partner(p, c):
        remote(wall.at[cut(c, p)], wall.at[cut(c, p)], last_s, last_r, partner, col).start()

    near = (1, ny - 1) if ny == 4 else tuple(range(1, ny))
    far = (2,) if ny == 4 else ()

    def pass_near(p, c, axis, d):
        if far:
            to = along(p, ny - d, 0) if axis == 0 else along(p, 0, ny - d)
            send_part(cut_half(c, p, 0 if d == 1 else 1), p, c, to)

    def spread_second(p, c):
        for d in near:
            send_part(cut(c, p), p, c, along(p, 0, d))

    def arrived(p, a, b):
        c = along(p, a, b)
        await_recv(wall.at[cut(c, p)], wall_r.at[p, c])
        return c

    write = pltpu.make_async_copy(right_out, wall.at[:, columns_of(col)], out_sem)
    write.start()
    for p in range(2):
        for d in near:
            send_own(p, along(p, d, 0))
    for p in range(2):
        for d in near:
            send_own(p, along(p, 0, d))
    for dz, dy in offsets:
        remote(squares.at[col, pl.ds(0, 1)], squares.at[col, pl.ds(0, 1)], sq_s, sq_r, row, shifted(dz, dy)).start()
    high, low = split(linv[...])
    ortho[...] = (mm(left[...], high, NT) + mm(left[...], low, NT)).astype(BF16)
    for a in near:
        for p in range(2):
            c = arrived(p, a, 0)
            pass_near(p, c, 0, a)
            spread_second(p, c)
            to_partner(p, c)
    for b in near:
        for p in range(2):
            c = arrived(p, 0, b)
            pass_near(p, c, 1, b)
            to_partner(p, c)
    for a in far:
        for p in range(2):
            c = arrived(p, a, 0)
            spread_second(p, c)
            to_partner(p, c)
    await_recv(squares.at[pl.ds(0, n_col - 1), pl.ds(0, 1)], sq_r)
    await_send(squares.at[pl.ds(0, n_col - 1), pl.ds(0, 1)], sq_s)
    norm = jnp.sqrt(jnp.sum(squares[:, 0:1, :], axis=0) + 1e-06)
    basis_out[...] = rightf[...] / norm
    for r in range(rounds):
        o2_out[r * ROUND : (r + 1) * ROUND, :] = (ortho[row_of(r, col), :].astype(F32) * (factor / norm)).astype(BF16)
    for a in near:
        for b in near:
            for p in range(2):
                c = arrived(p, a, b)
                pass_near(p, c, 1, b)
                to_partner(p, c)
    ortho_out[...] = mm(perm_t[...], ortho[...]).astype(BF16)
    for b in far:
        for p in range(2):
            to_partner(p, arrived(p, 0, b))
    for a in far:
        for b in near:
            for p in range(2):
                c = arrived(p, a, b)
                pass_near(p, c, 1, b)
                to_partner(p, c)
    for a in near + far:
        for b in far:
            for p in range(2):
                to_partner(p, arrived(p, a, b))
    most = pl.ds(0, 2 * rank_part), pl.ds(0, (n_col - 1) * tile_cols)
    await_recv(wall.at[most], last_r)
    await_send(wall.at[most], last_s)
    await_send(wall.at[most], wall_s)
    store.wait()
    write.wait()


def output_kernel(
    parts, o2, ortho, right, merged, basis, wall, new_momentum, update, new_basis, wall_v, sum_v, update_v, in_sem, out_sem
):
    flat, cols = update.shape
    tile_rows = merged.shape[0]
    some_rows, some_cols = tile_rows // parts, cols // parts
    loads, stores = [], [pltpu.make_async_copy(basis, new_basis, out_sem.at[2, 0])]
    for i in range(parts):
        at, of = pl.ds(i * some_rows, some_rows), pl.ds(i * some_cols, some_cols)
        loads.append(pltpu.make_async_copy(wall.at[:, of], wall_v.at[:, of], in_sem.at[i]))
        stores.append(pltpu.make_async_copy(sum_v.at[at, :], new_momentum.at[at, :], out_sem.at[0, i]))
        stores.append(pltpu.make_async_copy(update_v.at[:, of], update.at[:, of], out_sem.at[1, i]))
    for load in loads:
        load.start()
    stores[0].start()
    for i in range(parts):
        at, of = pl.ds(i * some_rows, some_rows), pl.ds(i * some_cols, some_cols)
        fed_back = mm(ortho[at, :], right[...])
        sum_v[at, :] = (merged[at, :].astype(F32) - 0.05 * fed_back).astype(BF16)
        stores[2 * i + 1].start()
        loads[i].wait()
        update_v[:, of] = mm(o2[...], wall_v[:, of]).astype(BF16)
        stores[2 * i + 2].start()
    for store in stores:
        store.wait()


def shards(nz, ny, nx, flat_grad, flat_rows, momentum, basis):
    tile_rows, tile_cols = momentum.shape
    flat, cols = flat_grad.shape
    rank = basis.shape[1]
    n_col, n_row = nz * ny, nx * CORES
    piece = tile_cols // n_row
    half = tile_cols // CORES
    factor = math.sqrt(tile_rows * n_row * cols / rank)
    dma = pltpu.SemaphoreType.DMA
    any_space = pl.BlockSpec(memory_space=pl.ANY)
    vmem = pl.BlockSpec(memory_space=pltpu.VMEM)
    hbm = pl.BlockSpec(memory_space=pltpu.HBM)
    shape = jax.ShapeDtypeStruct
    merged, ortho, right, new_basis, o2, wall = pl.pallas_call(
        functools.partial(main_kernel, nz, ny, nx, factor),
        out_shape=[
            shape((tile_rows, tile_cols), BF16),
            shape((tile_rows, rank), BF16),
            shape((rank, tile_cols), BF16),
            shape((tile_cols, rank), F32),
            shape((flat, rank), BF16),
            shape((rank, cols), BF16),
        ],
        in_specs=[hbm, hbm, hbm, hbm],
        out_specs=[any_space, vmem, vmem, vmem, vmem, any_space],
        scratch_shapes=[
            pltpu.VMEM((tile_rows, tile_cols), BF16),
            pltpu.VMEM((tile_rows, tile_cols), BF16),
            pltpu.VMEM((tile_rows, tile_cols), BF16),
            pltpu.VMEM((tile_cols, tile_rows), BF16),
            pltpu.VMEM((tile_rows, tile_rows), BF16),
            pltpu.VMEM((tile_rows, tile_rows), BF16),
            pltpu.VMEM((1, flat), jnp.int32),
            pltpu.VMEM((n_col, 8, 128), jnp.int32),
            pltpu.VMEM((tile_cols, rank), BF16),
            pltpu.VMEM((tile_rows, rank), BF16),
            pltpu.VMEM(((n_col - 1) * flat, rank), BF16),
            pltpu.VMEM((tile_rows, rank), BF16),
            pltpu.VMEM((rank, rank), F32),
            pltpu.VMEM((rank, rank), F32),
            pltpu.VMEM((nx, rank // CORES, rank), F32),
            pltpu.VMEM((rank, rank), F32),
            pltpu.VMEM((half, rank), BF16),
            pltpu.VMEM((half, rank), BF16),
            pltpu.VMEM((half, rank), BF16),
            pltpu.VMEM(((nx - 1) * piece, rank), BF16),
            pltpu.VMEM((tile_cols, rank), BF16),
            pltpu.VMEM((tile_cols, rank), F32),
            pltpu.VMEM((n_col, 8, rank), F32),
            pltpu.VMEM((tile_cols, rank), F32),
            pltpu.VMEM((tile_rows, rank), BF16),
            pltpu.VMEM((rank, rank), F32),
            pltpu.VMEM((rank, rank), F32),
            pltpu.VMEM((rank, rank), F32),
            dma, dma,
            dma, dma,
            dma, dma((flat // ROUND,)),
            dma((CHUNKS,)), dma((CHUNKS,)), dma, dma, dma((CHUNKS,)), dma((CHUNKS,)),
            dma, dma, dma((2,)), dma((2,)), dma, dma((nx,)),
            dma, dma((2, n_col)),
            dma, dma,
            dma((2,)), dma((2,)),
            dma((flat // ROUND,)),
            dma, dma,
        ],
        compiler_params=pltpu.CompilerParams(
            collective_id=0, has_side_effects=True, vmem_limit_bytes=42 * 1024 * 1024
        ),
        name="dion_main",
    )(flat_grad, flat_rows.reshape(1, flat), momentum, basis)

    parts = 8
    new_momentum, update, new_basis = pl.pallas_call(
        functools.partial(output_kernel, parts),
        out_shape=[
            shape((tile_rows, tile_cols), BF16),
            shape((flat, cols), BF16),
            shape((tile_cols, rank), F32),
        ],
        in_specs=[vmem, vmem, vmem, vmem, vmem, any_space],
        out_specs=[any_space, any_space, any_space],
        scratch_shapes=[
            pltpu.VMEM((rank, cols), BF16),
            pltpu.VMEM((tile_rows, tile_cols), BF16),
            pltpu.VMEM((flat, cols), BF16),
            dma((parts,)),
            dma((3, parts)),
        ],
        compiler_params=pltpu.CompilerParams(vmem_limit_bytes=44 * 1024 * 1024),
        name="dion_outputs",
    )(o2, ortho, right, merged, new_basis, wall)
    return new_momentum, new_basis, update


def solution(mesh):
    n_row, n_col = mesh.shape["row"], mesh.shape["col"]
    ny = math.isqrt(n_col)
    return jax.shard_map(
        functools.partial(shards, n_col // ny, ny, n_row // CORES),
        mesh=mesh,
        in_specs=(P(("row", "col"), None), P(("row", "col")), P("row", "col"), P("col", None)),
        out_specs=(P("row", "col"), P("col", None), P(("row", "col"), None)),
        check_vma=False,
    )
```

```python
import functools
import math

import jax
import jax.numpy as jnp
from jax import lax
from jax.experimental import pallas as pl
from jax.experimental.pallas import tpu as pltpu
from jax.sharding import PartitionSpec as P

ITERS = 4
CORES = 2
STEP = 16
ROUND = 32
CHUNKS = 3
MESH = pl.DeviceIdType.MESH
BF16 = jnp.bfloat16
F32 = jnp.float32
NN = (((1,), (0,)), ((), ()))
NT = (((1,), (1,)), ((), ()))
TN = (((0,), (0,)), ((), ()))


def mm(a, b, dims=NN):
    return lax.dot_general(a, b, dims, preferred_element_type=F32)


def split(a):
    high = a.astype(BF16)
    return high, (a - high.astype(F32)).astype(BF16)


def main_kernel(
    nz, ny, nx, factor,
    grad, slots_in, mom, basis,
    merged_out, ortho_out, right_out, basis_out, o2_out, wall,
    momv, recv, merged, turned, perm, perm_t, named_in, slots, current, rs_send, rs_recv, left, gram_own, gram_pair, gram_x, gram_all, w_send, w_pair, w_mid, w_recv, wag,
    w_sum, squares, rightf, ortho, amat, xmat, linv, mom_sem, out_sem, slot_s, slot_r, grad_s, grad_r,
    rs_s, rs_r, sq_s, sq_r, ag_s, ag_r, gram_s, gram_r, wrs_s, wrs_r, wag_s, wag_r, wall_s, wall_r, pair_s, pair_r,
    half_s, half_r, own_sem, last_s, last_r,
):
    row, col = lax.axis_index("row"), lax.axis_index("col")
    z, y = col // ny, col % ny
    x, core = row // CORES, row % CORES
    n_col, n_row = nz * ny, nx * CORES
    tile_rows, tile_cols = merged.shape
    rank = current.shape[1]
    flat = tile_rows // n_col
    rounds, per_round = flat // ROUND, n_col * ROUND
    group = flat * ny
    piece = tile_cols // n_row
    quarter = tile_cols // 4
    half = tile_cols // CORES
    offsets = [(dz, dy) for dz in range(nz) for dy in range(ny) if (dz, dy) != (0, 0)]
    offsets.sort(key=lambda o: (min(o[0], nz - o[0]) + min(o[1], ny - o[1]), max(o)))
    far_first = offsets[::-1]
    across = sorted(range(1, nx), key=lambda d: -min(d, nx - d))
    partner = x * CORES + (1 - core)

    def shifted(dz, dy):
        return lax.rem(z + dz, nz) * ny + lax.rem(y + dy, ny)

    def beside(dx):
        return lax.rem(x + dx, nx) * CORES + core

    def rows_at(index, size):
        return pl.ds(pl.multiple_of(index * size, size), size)

    def remote(src, dst, send, receive, to_row, to_col):
        return pltpu.make_async_remote_copy(
            src_ref=src, dst_ref=dst, send_sem=send, recv_sem=receive, device_id=(to_row, to_col), device_id_type=MESH
        )

    def await_recv(ref, sem):
        remote(ref, ref, sem, sem, partner, col).wait_recv()

    def await_send(ref, sem):
        remote(ref, ref, sem, sem, partner, col).wait_send()

    load = pltpu.make_async_copy(mom, momv, mom_sem)
    load.start()
    load_basis = pltpu.make_async_copy(basis, rightf, half_s.at[0])
    load_basis.start()
    load_slots = pltpu.make_async_copy(slots_in, named_in, half_s.at[1])
    load_slots.start()
    squares[...] = jnp.zeros_like(squares)

    barrier = pltpu.get_barrier_semaphore()
    for dz, dy in offsets:
        pl.semaphore_signal(barrier, inc=1, device_id=(row, shifted(dz, dy)), device_id_type=MESH)
    for dx in range(1, nx):
        pl.semaphore_signal(barrier, inc=1, device_id=(beside(dx), col), device_id_type=MESH)
    pl.semaphore_signal(barrier, inc=1, device_id=(partner, col), device_id_type=MESH)
    pl.semaphore_wait(barrier, n_col - 1 + nx)

    slots[col] = jnp.zeros((8, 128), jnp.int32)
    load_slots.wait()
    slots[col, 0:1, 0:flat] = named_in[...]
    for dz, dy in offsets:
        remote(slots.at[col], slots.at[col], slot_s, slot_r, row, shifted(dz, dy)).start()

    def columns_of(c):
        return pl.ds(pl.multiple_of(c * tile_cols, 128), tile_cols)

    def row_of(r, c):
        return pl.ds(pl.multiple_of(r * per_round + c * ROUND, ROUND), ROUND)

    own = []
    for r in range(rounds):
        taken = pl.ds(r * ROUND, ROUND)
        for dz, dy in offsets:
            to = shifted(dz, dy)
            remote(
                grad.at[taken, columns_of(to)], recv.at[row_of(r, col), :], grad_s, grad_r.at[r], row, to
            ).start()
        own.append(
            pltpu.make_async_copy(grad.at[taken, columns_of(col)], recv.at[row_of(r, col), :], own_sem.at[r])
        )
        own[r].start()

    load_basis.wait()
    current[...] = rightf[...].astype(BF16)
    await_recv(slots.at[pl.ds(0, n_col - 1)], slot_r)
    await_send(slots.at[pl.ds(0, n_col - 1)], slot_s)

    def fill_perm(c, _):
        named = jnp.broadcast_to(slots[c][0:1, :], (128, 128)).T - row * tile_rows
        lanes = lax.broadcasted_iota(jnp.int32, (ROUND, 128), 1)
        for r in range(rounds):
            part = named[r * ROUND : (r + 1) * ROUND]
            for t in range(tile_rows // 128):
                perm[row_of(r, c), t * 128 : (t + 1) * 128] = jnp.where(part == lanes + t * 128, 1.0, 0.0).astype(BF16)
        return 0

    lax.fori_loop(0, n_col, fill_perm, 0)
    load.wait()

    wide = 256
    n_wide, rest = tile_cols // wide, tile_cols % wide

    def permute(target, one, source, at):
        block = one[at, :]

        def part(t, _):
            cols = rows_at(t, wide)
            target[at, cols] = mm(block, source[:, cols]).astype(BF16)
            return 0

        lax.fori_loop(0, n_wide, part, 0)
        if rest:
            cols = pl.ds(n_wide * wide, rest)
            target[at, cols] = mm(block, source[:, cols]).astype(BF16)

    def permute_group(g, _):
        permute(merged, perm, momv, rows_at(g, group))
        return 0

    lax.fori_loop(0, nz, permute_group, 0)

    def turn_perm(t, _):
        cols = rows_at(t, 128)
        perm_t[cols, :] = perm[:, cols].T
        return 0

    lax.fori_loop(0, tile_rows // 128, turn_perm, 0)

    for r in range(rounds):
        begin = r * per_round
        own[r].wait()
        await_recv(recv.at[pl.ds(0, (n_col - 1) * ROUND), :], grad_r.at[r])

        def add(i, _, begin=begin):
            at = pl.ds(pl.multiple_of(begin + i * ROUND, ROUND), ROUND)
            merged[at, :] = (merged[at, :].astype(F32) + recv[at, :].astype(F32)).astype(BF16)
            return 0

        lax.fori_loop(0, n_col, add, 0)

        def turn(t, _, begin=begin):
            cols = rows_at(t, 128)
            turned[cols, begin : begin + per_round] = merged[begin : begin + per_round, cols].T
            return 0

        lax.fori_loop(0, tile_cols // 128, turn, 0)
    await_send(recv.at[pl.ds(0, (n_col - 1) * flat), :], grad_s)

    lane = lax.broadcasted_iota(jnp.int32, (STEP, rank), 1)
    sub = lax.broadcasted_iota(jnp.int32, (STEP, rank), 0)

    def eliminate(b, _):
        start = b * STEP
        at = rows_at(b, STEP)
        a, v = amat[at, :], xmat[at, :]
        spread = [
            jnp.broadcast_to(jnp.sum(jnp.where(lane == start + k, a, 0.0), axis=1, keepdims=True), (STEP, rank))
            for k in range(STEP)
        ]
        inverse = jnp.ones((STEP, rank), F32)
        for k in range(STEP):
            one_over = 1.0 / jnp.broadcast_to(spread[k][k : k + 1, :], (STEP, rank))
            inverse = jnp.where(sub == k, one_over, inverse)
            if k < STEP - 1:
                ratio = jnp.where(sub > k, spread[k] * one_over, 0.0)
                a = a - ratio * jnp.broadcast_to(a[k : k + 1, :], (STEP, rank))
                v = v - ratio * jnp.broadcast_to(v[k : k + 1, :], (STEP, rank))
                for j in range(k + 1, STEP):
                    spread[j] = spread[j] - ratio * jnp.broadcast_to(spread[j][k : k + 1, :], (STEP, rank))
        linv[at, :] = v * jnp.sqrt(inverse)
        scaled = jnp.where(lane >= start + STEP, a * inverse, 0.0)
        change = lax.dot_general(
            scaled,
            jnp.concatenate([a, v], axis=1),
            TN,
            precision=lax.Precision.HIGHEST,
            preferred_element_type=F32,
        )
        amat[...] -= change[:, :rank]
        xmat[...] -= change[:, rank:]
        return 0

    steps = rank // STEP
    chunk, share = tile_rows // CHUNKS, flat // CHUNKS
    restored = tile_rows // (2 * ITERS)

    def share_of(h, c):
        return pl.ds(pl.multiple_of(h * chunk + c * share, share), share)

    def others(ref, h):
        return ref.at[pl.ds(h * (n_col - 1) * share, (n_col - 1) * share), :]

    gram_half = rank // CORES
    core_rows = rows_at(core, half)
    other_rows = rows_at(1 - core, half)

    def iterate(k, _):
        for h in range(CHUNKS):
            at = slice(h * chunk, (h + 1) * chunk)
            rs_send[at, :] = mm(merged[at, :], current[...]).astype(BF16)
            for i, (dz, dy) in enumerate(far_first):
                to = shifted(dz, dy)
                slot = pl.ds((h * (n_col - 1) + i) * share, share)
                remote(rs_send.at[share_of(h, to), :], rs_recv.at[slot, :], rs_s.at[h], rs_r.at[h], row, to).start()
            if h == 0:
                for dz, dy in offsets:
                    to = shifted(dz, dy)
                    remote(squares.at[col, pl.ds(0, 1)], squares.at[col, pl.ds(0, 1)], sq_s, sq_r, row, to).start()
        permute(momv, perm_t, merged, rows_at(2 * k, restored))
        await_recv(squares.at[pl.ds(0, n_col - 1), pl.ds(0, 1)], sq_r)
        norm = jnp.sqrt(jnp.sum(squares[:, 0:1, :], axis=0) + 1e-06)
        scale = 1.0 / jnp.where(k == 0, jnp.ones_like(norm), norm)
        for h in range(CHUNKS):
            await_recv(others(rs_recv, h), rs_r.at[h])
            total = rs_send[share_of(h, col), :].astype(F32)
            for i in range(n_col - 1):
                begin = (h * (n_col - 1) + i) * share
                total = total + rs_recv[begin : begin + share, :].astype(F32)
            left[share_of(h, col), :] = (total * scale).astype(BF16)
            for dz, dy in far_first:
                ours = left.at[share_of(h, col), :]
                remote(ours, ours, ag_s.at[h], ag_r.at[h], row, shifted(dz, dy)).start()
        xmat[...] = jnp.where(
            lax.broadcasted_iota(jnp.int32, (rank, rank), 0) == lax.broadcasted_iota(jnp.int32, (rank, rank), 1), 1.0, 0.0
        )
        await_send(squares.at[pl.ds(0, n_col - 1), pl.ds(0, 1)], sq_s)
        for h in range(CHUNKS):
            await_send(others(rs_recv, h), rs_s.at[h])

        for h in range(CHUNKS):
            at = slice(h * chunk, (h + 1) * chunk)
            await_recv(others(rs_recv, h), ag_r.at[h])
            gram_part = mm(left[at, :], left[at, :], TN)
            gram_own[...] = gram_part if h == 0 else gram_own[...] + gram_part
            if h < CHUNKS - 1:
                w_part = mm(turned[:, at], left[at, :])
                w_sum[...] = w_part if h == 0 else w_sum[...] + w_part
        final = slice((CHUNKS - 1) * chunk, CHUNKS * chunk)
        to_pair = remote(gram_own, gram_pair, gram_s, gram_r, partner, col)
        to_pair.start()
        w_send[...] = (w_sum[other_rows, :] + mm(turned[other_rows, final], left[final, :])).astype(BF16)
        w_to_pair = remote(w_send, w_pair, wrs_s.at[0], wrs_r.at[0], partner, col)
        w_to_pair.start()
        await_recv(gram_pair, gram_r)
        gram_rows = rows_at(core, gram_half)
        gram_x[x] = gram_own[gram_rows, :] + gram_pair[gram_rows, :]
        for dx in across:
            remote(gram_x.at[x], gram_x.at[x], half_s.at[0], half_r.at[0], beside(dx), col).start()
        own_half = w_sum[core_rows, :] + mm(turned[core_rows, final], left[final, :])
        await_recv(w_pair, wrs_r.at[0])
        w_mid[...] = (own_half + w_pair[...].astype(F32)).astype(BF16)
        for dx in across:
            to = lax.rem(x + dx, nx)
            slot = pl.ds((dx - 1) * piece, piece)
            remote(w_mid.at[rows_at(to, piece), :], w_recv.at[slot, :], wrs_s.at[1], wrs_r.at[1], beside(dx), col).start()
        for h in range(CHUNKS):
            await_send(others(rs_recv, h), ag_s.at[h])
        permute(momv, perm_t, merged, rows_at(2 * k + 1, restored))
        await_recv(gram_x.at[pl.ds(0, nx - 1)], half_r.at[0])
        gram = gram_x[0]
        for d in range(1, nx):
            gram = gram + gram_x[d]
        gram_all[gram_rows, :] = gram
        halves = remote(gram_all.at[gram_rows, :], gram_all.at[gram_rows, :], half_s.at[1], half_r.at[1], partner, col)
        halves.start()
        await_recv(gram_all.at[gram_rows, :], half_r.at[1])
        amat[...] = gram_all[...]
        lax.fori_loop(0, 1, eliminate, 0)
        await_recv(w_recv, wrs_r.at[1])
        total = w_mid[rows_at(x, piece), :].astype(F32)
        for d in range(nx - 1):
            total = total + w_recv[d * piece : (d + 1) * piece, :].astype(F32)

        def held(xc):
            return rows_at(core * nx + xc, piece)

        wag[held(x), :] = total.astype(BF16)
        for dx in across:
            remote(wag.at[held(x), :], wag.at[held(x), :], wag_s, wag_r.at[x], beside(dx), col).start()
        remote(wag.at[held(x), :], wag.at[held(x), :], pair_s, pair_r, partner, col).start()
        lax.fori_loop(1, steps - 1, eliminate, 0)
        for dx in range(1, nx):
            xc = lax.rem(x + dx, nx)
            await_recv(wag.at[held(xc), :], wag_r.at[xc])
            remote(wag.at[held(xc), :], wag.at[held(xc), :], pair_s, pair_r, partner, col).start()
        lax.fori_loop(steps - 1, steps, eliminate, 0)
        high, low = split(linv[...])

        def right_of(at):
            part = mm(wag[at, :], high, NT) + mm(wag[at, :], low, NT)
            rightf[at, :] = part
            current[at, :] = part.astype(BF16)
            return jnp.sum(part * part, axis=0, keepdims=True)

        summed = right_of(core_rows)
        to_pair.wait_send()
        w_to_pair.wait_send()
        await_send(gram_x.at[pl.ds(0, nx - 1)], half_s.at[0])
        halves.wait_send()
        await_send(w_recv, wrs_s.at[1])
        await_send(w_recv, wag_s)
        await_recv(w_pair, pair_r)
        summed = summed + right_of(other_rows)
        await_send(w_pair, pair_s)
        squares[col] = jnp.broadcast_to(summed, (8, rank))
        return 0

    lax.fori_loop(0, ITERS, iterate, 0)

    store = pltpu.make_async_copy(momv, merged_out, mom_sem)
    store.start()

    def turn_right(t, _):
        at = rows_at(t, 128)
        right_out[:, at] = current[at, :].T
        return 0

    lax.fori_loop(0, tile_cols // 128, turn_right, 0)

    rank_part = rank // 4

    def cut(c, p):
        return pl.ds(pl.multiple_of((core * 2 + p) * rank_part, rank_part), rank_part), columns_of(c)

    def cut_half(c, p, h):
        size = rank_part // 2
        return pl.ds(pl.multiple_of((core * 2 + p) * rank_part + h * size, size), size), columns_of(c)

    def along(p, a, b):
        return shifted(a, b) if p == 0 else shifted(b, a)

    def send_own(p, to):
        part, cols = cut(col, p)
        remote(right_out.at[part, :], wall.at[part, cols], wall_s, wall_r.at[p, col], row, to).start()

    def send_part(at, p, c, to):
        remote(wall.at[at], wall.at[at], wall_s, wall_r.at[p, c], row, to).start()

    def to_partner(p, c):
        remote(wall.at[cut(c, p)], wall.at[cut(c, p)], last_s, last_r, partner, col).start()

    near = (1, ny - 1) if ny == 4 else tuple(range(1, ny))
    far = (2,) if ny == 4 else ()

    def pass_near(p, c, axis, d):
        if far:
            to = along(p, ny - d, 0) if axis == 0 else along(p, 0, ny - d)
            send_part(cut_half(c, p, 0 if d == 1 else 1), p, c, to)

    def spread_second(p, c):
        for d in near:
            send_part(cut(c, p), p, c, along(p, 0, d))

    def arrived(p, a, b):
        c = along(p, a, b)
        await_recv(wall.at[cut(c, p)], wall_r.at[p, c])
        return c

    write = pltpu.make_async_copy(right_out, wall.at[:, columns_of(col)], out_sem)
    write.start()
    for p in range(2):
        for d in near:
            send_own(p, along(p, d, 0))
    for p in range(2):
        for d in near:
            send_own(p, along(p, 0, d))
    for dz, dy in offsets:
        remote(squares.at[col, pl.ds(0, 1)], squares.at[col, pl.ds(0, 1)], sq_s, sq_r, row, shifted(dz, dy)).start()
    high, low = split(linv[...])
    ortho[...] = (mm(left[...], high, NT) + mm(left[...], low, NT)).astype(BF16)
    for a in near:
        for p in range(2):
            c = arrived(p, a, 0)
            pass_near(p, c, 0, a)
            spread_second(p, c)
            to_partner(p, c)
    for b in near:
        for p in range(2):
            c = arrived(p, 0, b)
            pass_near(p, c, 1, b)
            to_partner(p, c)
    for a in far:
        for p in range(2):
            c = arrived(p, a, 0)
            spread_second(p, c)
            to_partner(p, c)
    await_recv(squares.at[pl.ds(0, n_col - 1), pl.ds(0, 1)], sq_r)
    await_send(squares.at[pl.ds(0, n_col - 1), pl.ds(0, 1)], sq_s)
    norm = jnp.sqrt(jnp.sum(squares[:, 0:1, :], axis=0) + 1e-06)
    basis_out[...] = rightf[...] / norm
    for r in range(rounds):
        o2_out[r * ROUND : (r + 1) * ROUND, :] = (ortho[row_of(r, col), :].astype(F32) * (factor / norm)).astype(BF16)
    for a in near:
        for b in near:
            for p in range(2):
                c = arrived(p, a, b)
                pass_near(p, c, 1, b)
                to_partner(p, c)
    ortho_out[...] = mm(perm_t[...], ortho[...]).astype(BF16)
    for b in far:
        for p in range(2):
            to_partner(p, arrived(p, 0, b))
    for a in far:
        for b in near:
            for p in range(2):
                c = arrived(p, a, b)
                pass_near(p, c, 1, b)
                to_partner(p, c)
    for a in near + far:
        for b in far:
            for p in range(2):
                to_partner(p, arrived(p, a, b))
    most = pl.ds(0, 2 * rank_part), pl.ds(0, (n_col - 1) * tile_cols)
    await_recv(wall.at[most], last_r)
    await_send(wall.at[most], last_s)
    await_send(wall.at[most], wall_s)
    store.wait()
    write.wait()


def output_kernel(
    parts, o2, ortho, right, merged, basis, wall, new_momentum, update, new_basis, wall_v, sum_v, update_v, in_sem, out_sem
):
    flat, cols = update.shape
    tile_rows = merged.shape[0]
    some_rows, some_cols = tile_rows // parts, cols // parts
    loads, stores = [], [pltpu.make_async_copy(basis, new_basis, out_sem.at[2, 0])]
    for i in range(parts):
        at, of = pl.ds(i * some_rows, some_rows), pl.ds(i * some_cols, some_cols)
        loads.append(pltpu.make_async_copy(wall.at[:, of], wall_v.at[:, of], in_sem.at[i]))
        stores.append(pltpu.make_async_copy(sum_v.at[at, :], new_momentum.at[at, :], out_sem.at[0, i]))
        stores.append(pltpu.make_async_copy(update_v.at[:, of], update.at[:, of], out_sem.at[1, i]))
    for load in loads:
        load.start()
    stores[0].start()
    for i in range(parts):
        at, of = pl.ds(i * some_rows, some_rows), pl.ds(i * some_cols, some_cols)
        fed_back = mm(ortho[at, :], right[...])
        sum_v[at, :] = (merged[at, :].astype(F32) - 0.05 * fed_back).astype(BF16)
        stores[2 * i + 1].start()
        loads[i].wait()
        update_v[:, of] = mm(o2[...], wall_v[:, of]).astype(BF16)
        stores[2 * i + 2].start()
    for store in stores:
        store.wait()


def shards(nz, ny, nx, flat_grad, flat_rows, momentum, basis):
    tile_rows, tile_cols = momentum.shape
    flat, cols = flat_grad.shape
    rank = basis.shape[1]
    n_col, n_row = nz * ny, nx * CORES
    piece = tile_cols // n_row
    half = tile_cols // CORES
    factor = math.sqrt(tile_rows * n_row * cols / rank)
    dma = pltpu.SemaphoreType.DMA
    any_space = pl.BlockSpec(memory_space=pl.ANY)
    vmem = pl.BlockSpec(memory_space=pltpu.VMEM)
    hbm = pl.BlockSpec(memory_space=pltpu.HBM)
    shape = jax.ShapeDtypeStruct
    merged, ortho, right, new_basis, o2, wall = pl.pallas_call(
        functools.partial(main_kernel, nz, ny, nx, factor),
        out_shape=[
            shape((tile_rows, tile_cols), BF16),
            shape((tile_rows, rank), BF16),
            shape((rank, tile_cols), BF16),
            shape((tile_cols, rank), F32),
            shape((flat, rank), BF16),
            shape((rank, cols), BF16),
        ],
        in_specs=[hbm, hbm, hbm, hbm],
        out_specs=[any_space, vmem, vmem, vmem, vmem, any_space],
        scratch_shapes=[
            pltpu.VMEM((tile_rows, tile_cols), BF16),
            pltpu.VMEM((tile_rows, tile_cols), BF16),
            pltpu.VMEM((tile_rows, tile_cols), BF16),
            pltpu.VMEM((tile_cols, tile_rows), BF16),
            pltpu.VMEM((tile_rows, tile_rows), BF16),
            pltpu.VMEM((tile_rows, tile_rows), BF16),
            pltpu.VMEM((1, flat), jnp.int32),
            pltpu.VMEM((n_col, 8, 128), jnp.int32),
            pltpu.VMEM((tile_cols, rank), BF16),
            pltpu.VMEM((tile_rows, rank), BF16),
            pltpu.VMEM(((n_col - 1) * flat, rank), BF16),
            pltpu.VMEM((tile_rows, rank), BF16),
            pltpu.VMEM((rank, rank), F32),
            pltpu.VMEM((rank, rank), F32),
            pltpu.VMEM((nx, rank // CORES, rank), F32),
            pltpu.VMEM((rank, rank), F32),
            pltpu.VMEM((half, rank), BF16),
            pltpu.VMEM((half, rank), BF16),
            pltpu.VMEM((half, rank), BF16),
            pltpu.VMEM(((nx - 1) * piece, rank), BF16),
            pltpu.VMEM((tile_cols, rank), BF16),
            pltpu.VMEM((tile_cols, rank), F32),
            pltpu.VMEM((n_col, 8, rank), F32),
            pltpu.VMEM((tile_cols, rank), F32),
            pltpu.VMEM((tile_rows, rank), BF16),
            pltpu.VMEM((rank, rank), F32),
            pltpu.VMEM((rank, rank), F32),
            pltpu.VMEM((rank, rank), F32),
            dma, dma,
            dma, dma,
            dma, dma((flat // ROUND,)),
            dma((CHUNKS,)), dma((CHUNKS,)), dma, dma, dma((CHUNKS,)), dma((CHUNKS,)),
            dma, dma, dma((2,)), dma((2,)), dma, dma((nx,)),
            dma, dma((2, n_col)),
            dma, dma,
            dma((2,)), dma((2,)),
            dma((flat // ROUND,)),
            dma, dma,
        ],
        compiler_params=pltpu.CompilerParams(
            collective_id=0, has_side_effects=True, vmem_limit_bytes=42 * 1024 * 1024
        ),
        name="dion_main",
    )(flat_grad, flat_rows.reshape(1, flat), momentum, basis)

    parts = 8
    new_momentum, update, new_basis = pl.pallas_call(
        functools.partial(output_kernel, parts),
        out_shape=[
            shape((tile_rows, tile_cols), BF16),
            shape((flat, cols), BF16),
            shape((tile_cols, rank), F32),
        ],
        in_specs=[vmem, vmem, vmem, vmem, vmem, any_space],
        out_specs=[any_space, any_space, any_space],
        scratch_shapes=[
            pltpu.VMEM((rank, cols), BF16),
            pltpu.VMEM((tile_rows, tile_cols), BF16),
            pltpu.VMEM((flat, cols), BF16),
            dma((parts,)),
            dma((3, parts)),
        ],
        compiler_params=pltpu.CompilerParams(vmem_limit_bytes=44 * 1024 * 1024),
        name="dion_outputs",
    )(o2, ortho, right, merged, new_basis, wall)
    return new_momentum, new_basis, update


def solution(mesh):
    n_row, n_col = mesh.shape["row"], mesh.shape["col"]
    ny = math.isqrt(n_col)
    return jax.shard_map(
        functools.partial(shards, n_col // ny, ny, n_row // CORES),
        mesh=mesh,
        in_specs=(P(("row", "col"), None), P(("row", "col")), P("row", "col"), P("col", None)),
        out_specs=(P("row", "col"), P("col", None), P(("row", "col"), None)),
        check_vma=False,
    )
```

```python
import functools
import math

import jax
import jax.numpy as jnp
from jax import lax
from jax.experimental import pallas as pl
from jax.experimental.pallas import tpu as pltpu
from jax.sharding import PartitionSpec as P

ITERS = 4
CORES = 2
STEP = 32
ROUND = 32
CHUNKS = 3
MESH = pl.DeviceIdType.MESH
BF16 = jnp.bfloat16
F32 = jnp.float32
NN = (((1,), (0,)), ((), ()))
NT = (((1,), (1,)), ((), ()))
TN = (((0,), (0,)), ((), ()))


def mm(a, b, dims=NN):
    return lax.dot_general(a, b, dims, preferred_element_type=F32)


def split(a):
    high = a.astype(BF16)
    return high, (a - high.astype(F32)).astype(BF16)


def main_kernel(
    nz, ny, nx, factor,
    grad, slots_in, mom, basis,
    merged_out, ortho_out, right_out, basis_out, o2_out, wall,
    momv, recv, merged, turned, perm, perm_t, named_in, slots, current, rs_send, rs_recv, left, gram_own, gram_pair, gram_x, gram_all, w_send, w_pair, w_mid, w_recv, wag,
    w_sum, squares, rightf, ortho, amat, xmat, linv, mom_sem, out_sem, slot_s, slot_r, grad_s, grad_r,
    rs_s, rs_r, sq_s, sq_r, ag_s, ag_r, gram_s, gram_r, wrs_s, wrs_r, xrs_s, xrs_r, wag_s, wag_r, wall_s, wall_r, pair_s, pair_r,
    half_s, half_r, own_sem, last_s, last_r,
):
    row, col = lax.axis_index("row"), lax.axis_index("col")
    z, y = col // ny, col % ny
    x, core = row // CORES, row % CORES
    n_col, n_row = nz * ny, nx * CORES
    tile_rows, tile_cols = merged.shape
    rank = current.shape[1]
    flat = tile_rows // n_col
    rounds, per_round = flat // ROUND, n_col * ROUND
    group = flat * ny
    piece = tile_cols // n_row
    quarter = tile_cols // 4
    half = tile_cols // CORES
    offsets = [(dz, dy) for dz in range(nz) for dy in range(ny) if (dz, dy) != (0, 0)]
    offsets.sort(key=lambda o: (min(o[0], nz - o[0]) + min(o[1], ny - o[1]), max(o)))
    far_first = offsets[::-1]
    across = sorted(range(1, nx), key=lambda d: -min(d, nx - d))
    partner = x * CORES + (1 - core)

    def shifted(dz, dy):
        return lax.rem(z + dz, nz) * ny + lax.rem(y + dy, ny)

    def beside(dx):
        return lax.rem(x + dx, nx) * CORES + core

    def rows_at(index, size):
        return pl.ds(pl.multiple_of(index * size, size), size)

    def remote(src, dst, send, receive, to_row, to_col):
        return pltpu.make_async_remote_copy(
            src_ref=src, dst_ref=dst, send_sem=send, recv_sem=receive, device_id=(to_row, to_col), device_id_type=MESH
        )

    def await_recv(ref, sem):
        remote(ref, ref, sem, sem, partner, col).wait_recv()

    def await_send(ref, sem):
        remote(ref, ref, sem, sem, partner, col).wait_send()

    load = pltpu.make_async_copy(mom, momv, mom_sem)
    load.start()
    load_basis = pltpu.make_async_copy(basis, rightf, half_s.at[0])
    load_basis.start()
    load_slots = pltpu.make_async_copy(slots_in, named_in, half_s.at[1])
    load_slots.start()
    squares[...] = jnp.zeros_like(squares)

    barrier = pltpu.get_barrier_semaphore()
    for dz, dy in offsets:
        pl.semaphore_signal(barrier, inc=1, device_id=(row, shifted(dz, dy)), device_id_type=MESH)
    for dx in range(1, nx):
        pl.semaphore_signal(barrier, inc=1, device_id=(beside(dx), col), device_id_type=MESH)
    pl.semaphore_signal(barrier, inc=1, device_id=(partner, col), device_id_type=MESH)
    pl.semaphore_wait(barrier, n_col - 1 + nx)

    slots[col] = jnp.zeros((8, 128), jnp.int32)
    load_slots.wait()
    slots[col, 0:1, 0:flat] = named_in[...]
    for dz, dy in offsets:
        remote(slots.at[col], slots.at[col], slot_s, slot_r, row, shifted(dz, dy)).start()

    def columns_of(c):
        return pl.ds(pl.multiple_of(c * tile_cols, 128), tile_cols)

    def row_of(r, c):
        return pl.ds(pl.multiple_of(r * per_round + c * ROUND, ROUND), ROUND)

    own = []
    for r in range(rounds):
        taken = pl.ds(r * ROUND, ROUND)
        for dz, dy in offsets:
            to = shifted(dz, dy)
            remote(
                grad.at[taken, columns_of(to)], recv.at[row_of(r, col), :], grad_s, grad_r.at[r], row, to
            ).start()
        own.append(
            pltpu.make_async_copy(grad.at[taken, columns_of(col)], recv.at[row_of(r, col), :], own_sem.at[r])
        )
        own[r].start()

    load_basis.wait()
    current[...] = rightf[...].astype(BF16)
    await_recv(slots.at[pl.ds(0, n_col - 1)], slot_r)
    await_send(slots.at[pl.ds(0, n_col - 1)], slot_s)

    def fill_perm(c, _):
        named = jnp.broadcast_to(slots[c][0:1, :], (128, 128)).T - row * tile_rows
        lanes = lax.broadcasted_iota(jnp.int32, (ROUND, 128), 1)
        for r in range(rounds):
            part = named[r * ROUND : (r + 1) * ROUND]
            for t in range(tile_rows // 128):
                perm[row_of(r, c), t * 128 : (t + 1) * 128] = jnp.where(part == lanes + t * 128, 1.0, 0.0).astype(BF16)
        return 0

    lax.fori_loop(0, n_col, fill_perm, 0)
    load.wait()

    wide = 256
    n_wide, rest = tile_cols // wide, tile_cols % wide

    def permute(target, one, source, at):
        block = one[at, :]

        def part(t, _):
            cols = rows_at(t, wide)
            target[at, cols] = mm(block, source[:, cols]).astype(BF16)
            return 0

        lax.fori_loop(0, n_wide, part, 0)
        if rest:
            cols = pl.ds(n_wide * wide, rest)
            target[at, cols] = mm(block, source[:, cols]).astype(BF16)

    def permute_group(g, _):
        permute(merged, perm, momv, rows_at(g, group))
        return 0

    lax.fori_loop(0, nz, permute_group, 0)

    def turn_perm(t, _):
        cols = rows_at(t, 128)
        perm_t[cols, :] = perm[:, cols].T
        return 0

    lax.fori_loop(0, tile_rows // 128, turn_perm, 0)

    for r in range(rounds):
        begin = r * per_round
        own[r].wait()
        await_recv(recv.at[pl.ds(0, (n_col - 1) * ROUND), :], grad_r.at[r])

        def add(i, _, begin=begin):
            at = pl.ds(pl.multiple_of(begin + i * ROUND, ROUND), ROUND)
            merged[at, :] = (merged[at, :].astype(F32) + recv[at, :].astype(F32)).astype(BF16)
            return 0

        lax.fori_loop(0, n_col, add, 0)

        def turn(t, _, begin=begin):
            cols = rows_at(t, 128)
            turned[cols, begin : begin + per_round] = merged[begin : begin + per_round, cols].T
            return 0

        lax.fori_loop(0, tile_cols // 128, turn, 0)
    await_send(recv.at[pl.ds(0, (n_col - 1) * flat), :], grad_s)

    lane = lax.broadcasted_iota(jnp.int32, (STEP, rank), 1)
    sub = lax.broadcasted_iota(jnp.int32, (STEP, rank), 0)

    def eliminate(b, _):
        start = b * STEP
        at = rows_at(b, STEP)
        a, v = amat[at, :], xmat[at, :]
        spread = [
            jnp.broadcast_to(jnp.sum(jnp.where(lane == start + k, a, 0.0), axis=1, keepdims=True), (STEP, rank))
            for k in range(STEP)
        ]
        inverse = jnp.ones((STEP, rank), F32)
        for k in range(STEP):
            one_over = 1.0 / jnp.broadcast_to(spread[k][k : k + 1, :], (STEP, rank))
            inverse = jnp.where(sub == k, one_over, inverse)
            if k < STEP - 1:
                ratio = jnp.where(sub > k, spread[k] * one_over, 0.0)
                a = a - ratio * jnp.broadcast_to(a[k : k + 1, :], (STEP, rank))
                v = v - ratio * jnp.broadcast_to(v[k : k + 1, :], (STEP, rank))
                for j in range(k + 1, STEP):
                    spread[j] = spread[j] - ratio * jnp.broadcast_to(spread[j][k : k + 1, :], (STEP, rank))
        linv[at, :] = v * jnp.sqrt(inverse)
        scaled = jnp.where(lane >= start + STEP, a * inverse, 0.0)
        change = lax.dot_general(
            scaled,
            jnp.concatenate([a, v], axis=1),
            TN,
            precision=lax.Precision.HIGHEST,
            preferred_element_type=F32,
        )
        amat[...] -= change[:, :rank]
        xmat[...] -= change[:, rank:]
        return 0

    steps = rank // STEP
    chunk, share = tile_rows // CHUNKS, flat // CHUNKS
    restored = tile_rows // (2 * ITERS)

    def share_of(h, c):
        return pl.ds(pl.multiple_of(h * chunk + c * share, share), share)

    def others(ref, h):
        return ref.at[pl.ds(h * (n_col - 1) * share, (n_col - 1) * share), :]

    gram_half = rank // CORES

    sizes = [(piece // 2 + 15) // 16 * 16]
    sizes.append(piece - sizes[0])
    PARTS = (0, 1)

    def half_rows(e, c):
        return pl.ds(pl.multiple_of(e * n_row * sizes[0] + c * nx * sizes[e], 16), nx * sizes[e])

    def held(e, xc):
        return pl.ds(pl.multiple_of(e * n_row * sizes[0] + (core * nx + xc) * sizes[e], 16), sizes[e])

    def mid_rows(e, xc):
        return pl.ds(pl.multiple_of(e * nx * sizes[0] + xc * sizes[e], 16), sizes[e])

    def mid_part(e):
        return pl.ds(e * nx * sizes[0], nx * sizes[e])

    def recv_rows(e, i):
        return pl.ds(e * (nx - 1) * sizes[0] + i * sizes[e], sizes[e])

    def recv_part(e):
        return pl.ds(e * (nx - 1) * sizes[0], (nx - 1) * sizes[e])


    def iterate(k, _):
        for h in range(CHUNKS):
            at = slice(h * chunk, (h + 1) * chunk)
            rs_send[at, :] = mm(merged[at, :], current[...]).astype(BF16)
            for i, (dz, dy) in enumerate(far_first):
                to = shifted(dz, dy)
                slot = pl.ds((h * (n_col - 1) + i) * share, share)
                remote(rs_send.at[share_of(h, to), :], rs_recv.at[slot, :], rs_s.at[h], rs_r.at[h], row, to).start()
            if h == 0:
                for dz, dy in offsets:
                    to = shifted(dz, dy)
                    remote(squares.at[col, pl.ds(0, 1)], squares.at[col, pl.ds(0, 1)], sq_s, sq_r, row, to).start()
        permute(momv, perm_t, merged, rows_at(2 * k, restored))
        await_recv(squares.at[pl.ds(0, n_col - 1), pl.ds(0, 1)], sq_r)
        norm = jnp.sqrt(jnp.sum(squares[:, 0:1, :], axis=0) + 1e-06)
        scale = 1.0 / jnp.where(k == 0, jnp.ones_like(norm), norm)
        for h in range(CHUNKS):
            await_recv(others(rs_recv, h), rs_r.at[h])
            total = rs_send[share_of(h, col), :].astype(F32)
            for i in range(n_col - 1):
                begin = (h * (n_col - 1) + i) * share
                total = total + rs_recv[begin : begin + share, :].astype(F32)
            left[share_of(h, col), :] = (total * scale).astype(BF16)
            for dz, dy in far_first:
                ours = left.at[share_of(h, col), :]
                remote(ours, ours, ag_s.at[h], ag_r.at[h], row, shifted(dz, dy)).start()
        xmat[...] = jnp.where(
            lax.broadcasted_iota(jnp.int32, (rank, rank), 0) == lax.broadcasted_iota(jnp.int32, (rank, rank), 1), 1.0, 0.0
        )
        await_send(squares.at[pl.ds(0, n_col - 1), pl.ds(0, 1)], sq_s)
        for h in range(CHUNKS):
            await_send(others(rs_recv, h), rs_s.at[h])

        for h in range(CHUNKS):
            at = slice(h * chunk, (h + 1) * chunk)
            await_recv(others(rs_recv, h), ag_r.at[h])
            gram_part = mm(left[at, :], left[at, :], TN)
            gram_own[...] = gram_part if h == 0 else gram_own[...] + gram_part
            if h < CHUNKS - 1:
                w_part = mm(turned[:, at], left[at, :])
                w_sum[...] = w_part if h == 0 else w_sum[...] + w_part
        final = slice((CHUNKS - 1) * chunk, CHUNKS * chunk)
        to_pair = remote(gram_own, gram_pair, gram_s, gram_r, partner, col)
        to_pair.start()
        w_to_pair = []
        for e in PARTS:
            at = half_rows(e, 1 - core)
            here = mid_part(e)
            w_send[here, :] = (w_sum[at, :] + mm(turned[at, final], left[final, :])).astype(BF16)
            w_to_pair.append(
                remote(w_send.at[here, :], w_pair.at[here, :], wrs_s.at[e], wrs_r.at[e], partner, col)
            )
            w_to_pair[e].start()
        await_recv(gram_pair, gram_r)
        gram_rows = rows_at(core, gram_half)
        gram_x[x] = gram_own[gram_rows, :] + gram_pair[gram_rows, :]
        for dx in across:
            remote(gram_x.at[x], gram_x.at[x], half_s.at[0], half_r.at[0], beside(dx), col).start()
        for e in PARTS:
            at = half_rows(e, core)
            here = mid_part(e)
            own_half = w_sum[at, :] + mm(turned[at, final], left[final, :])
            await_recv(w_pair.at[here, :], wrs_r.at[e])
            w_mid[here, :] = (own_half + w_pair[here, :].astype(F32)).astype(BF16)
            for dx in across:
                to = lax.rem(x + dx, nx)
                slot = w_recv.at[recv_rows(e, dx - 1), :]
                remote(w_mid.at[mid_rows(e, to), :], slot, xrs_s.at[e], xrs_r.at[e], beside(dx), col).start()
        for h in range(CHUNKS):
            await_send(others(rs_recv, h), ag_s.at[h])
        permute(momv, perm_t, merged, rows_at(2 * k + 1, restored))
        await_recv(gram_x.at[pl.ds(0, nx - 1)], half_r.at[0])
        gram = gram_x[0]
        for d in range(1, nx):
            gram = gram + gram_x[d]
        gram_all[gram_rows, :] = gram
        halves = remote(gram_all.at[gram_rows, :], gram_all.at[gram_rows, :], half_s.at[1], half_r.at[1], partner, col)
        halves.start()
        for e in PARTS:
            await_recv(w_recv.at[recv_part(e), :], xrs_r.at[e])
            total = w_mid[mid_rows(e, x), :].astype(F32)
            for d in range(nx - 1):
                total = total + w_recv[recv_rows(e, d), :].astype(F32)
            wag[held(e, x), :] = total.astype(BF16)
            ours = wag.at[held(e, x), :]
            for dx in across:
                remote(ours, ours, wag_s, wag_r.at[e, x], beside(dx), col).start()
            remote(ours, ours, pair_s, pair_r.at[e], partner, col).start()
            if e == 0:
                await_recv(gram_all.at[gram_rows, :], half_r.at[1])
                amat[...] = gram_all[...]
        lax.fori_loop(0, 2, eliminate, 0)
        for e in PARTS:
            for dx in range(1, nx):
                xc = lax.rem(x + dx, nx)
                theirs = wag.at[held(e, xc), :]
                await_recv(theirs, wag_r.at[e, xc])
                remote(theirs, theirs, pair_s, pair_r.at[e], partner, col).start()
            if e == 0:
                lax.fori_loop(2, steps - 1, eliminate, 0)
        lax.fori_loop(steps - 1, steps, eliminate, 0)

        high, low = split(linv[...])

        def right_of(at):
            part = mm(wag[at, :], high, NT) + mm(wag[at, :], low, NT)
            rightf[at, :] = part
            current[at, :] = part.astype(BF16)
            return jnp.sum(part * part, axis=0, keepdims=True)

        near_sum = right_of(half_rows(0, core)) + right_of(half_rows(1, core))
        to_pair.wait_send()
        for e in PARTS:
            w_to_pair[e].wait_send()
            await_send(w_recv.at[recv_part(e), :], xrs_s.at[e])
        await_send(gram_x.at[pl.ds(0, nx - 1)], half_s.at[0])
        halves.wait_send()
        await_send(w_recv, wag_s)
        far_sum = []
        for e in PARTS:
            await_recv(w_pair.at[mid_part(e), :], pair_r.at[e])
            far_sum.append(right_of(half_rows(e, 1 - core)))
        summed = near_sum + (far_sum[0] + far_sum[1])
        await_send(w_pair, pair_s)
        squares[col] = jnp.broadcast_to(summed, (8, rank))
        return 0

    lax.fori_loop(0, ITERS, iterate, 0)

    store = pltpu.make_async_copy(momv, merged_out, mom_sem)
    store.start()

    def turn_right(t, _):
        at = rows_at(t, 128)
        right_out[:, at] = current[at, :].T
        return 0

    lax.fori_loop(0, tile_cols // 128, turn_right, 0)

    rank_part = rank // 4

    def cut(c, p):
        return pl.ds(pl.multiple_of((core * 2 + p) * rank_part, rank_part), rank_part), columns_of(c)

    def cut_half(c, p, h):
        size = rank_part // 2
        return pl.ds(pl.multiple_of((core * 2 + p) * rank_part + h * size, size), size), columns_of(c)

    def along(p, a, b):
        return shifted(a, b) if p == 0 else shifted(b, a)

    def send_own(p, to):
        part, cols = cut(col, p)
        remote(right_out.at[part, :], wall.at[part, cols], wall_s, wall_r.at[p, col], row, to).start()

    def send_part(at, p, c, to):
        remote(wall.at[at], wall.at[at], wall_s, wall_r.at[p, c], row, to).start()

    def to_partner(p, c):
        remote(wall.at[cut(c, p)], wall.at[cut(c, p)], last_s, last_r, partner, col).start()

    near = (1, ny - 1) if ny == 4 else tuple(range(1, ny))
    far = (2,) if ny == 4 else ()

    def pass_near(p, c, axis, d):
        if far:
            to = along(p, ny - d, 0) if axis == 0 else along(p, 0, ny - d)
            send_part(cut_half(c, p, 0 if d == 1 else 1), p, c, to)

    def spread_second(p, c):
        for d in near:
            send_part(cut(c, p), p, c, along(p, 0, d))

    def arrived(p, a, b):
        c = along(p, a, b)
        await_recv(wall.at[cut(c, p)], wall_r.at[p, c])
        return c

    write = pltpu.make_async_copy(right_out, wall.at[:, columns_of(col)], out_sem)
    write.start()
    for p in range(2):
        for d in near:
            send_own(p, along(p, d, 0))
    for p in range(2):
        for d in near:
            send_own(p, along(p, 0, d))
    for dz, dy in offsets:
        remote(squares.at[col, pl.ds(0, 1)], squares.at[col, pl.ds(0, 1)], sq_s, sq_r, row, shifted(dz, dy)).start()
    high, low = split(linv[...])
    ortho[...] = (mm(left[...], high, NT) + mm(left[...], low, NT)).astype(BF16)
    for a in near:
        for p in range(2):
            c = arrived(p, a, 0)
            pass_near(p, c, 0, a)
            spread_second(p, c)
            to_partner(p, c)
    for b in near:
        for p in range(2):
            c = arrived(p, 0, b)
            pass_near(p, c, 1, b)
            to_partner(p, c)
    for a in far:
        for p in range(2):
            c = arrived(p, a, 0)
            spread_second(p, c)
            to_partner(p, c)
    await_recv(squares.at[pl.ds(0, n_col - 1), pl.ds(0, 1)], sq_r)
    await_send(squares.at[pl.ds(0, n_col - 1), pl.ds(0, 1)], sq_s)
    norm = jnp.sqrt(jnp.sum(squares[:, 0:1, :], axis=0) + 1e-06)
    basis_out[...] = rightf[...] / norm
    for r in range(rounds):
        o2_out[r * ROUND : (r + 1) * ROUND, :] = (ortho[row_of(r, col), :].astype(F32) * (factor / norm)).astype(BF16)
    for a in near:
        for b in near:
            for p in range(2):
                c = arrived(p, a, b)
                pass_near(p, c, 1, b)
                to_partner(p, c)
    ortho_out[...] = mm(perm_t[...], ortho[...]).astype(BF16)
    for b in far:
        for p in range(2):
            to_partner(p, arrived(p, 0, b))
    for a in far:
        for b in near:
            for p in range(2):
                c = arrived(p, a, b)
                pass_near(p, c, 1, b)
                to_partner(p, c)
    for a in near + far:
        for b in far:
            for p in range(2):
                to_partner(p, arrived(p, a, b))
    most = pl.ds(0, 2 * rank_part), pl.ds(0, (n_col - 1) * tile_cols)
    await_recv(wall.at[most], last_r)
    await_send(wall.at[most], last_s)
    await_send(wall.at[most], wall_s)
    store.wait()
    write.wait()


def output_kernel(
    parts, o2, ortho, right, merged, basis, wall, new_momentum, update, new_basis, wall_v, sum_v, update_v, in_sem, out_sem
):
    flat, cols = update.shape
    tile_rows = merged.shape[0]
    some_rows, some_cols = tile_rows // parts, cols // parts
    loads, stores = [], [pltpu.make_async_copy(basis, new_basis, out_sem.at[2, 0])]
    for i in range(parts):
        at, of = pl.ds(i * some_rows, some_rows), pl.ds(i * some_cols, some_cols)
        loads.append(pltpu.make_async_copy(wall.at[:, of], wall_v.at[:, of], in_sem.at[i]))
        stores.append(pltpu.make_async_copy(sum_v.at[at, :], new_momentum.at[at, :], out_sem.at[0, i]))
        stores.append(pltpu.make_async_copy(update_v.at[:, of], update.at[:, of], out_sem.at[1, i]))
    for load in loads:
        load.start()
    stores[0].start()
    for i in range(parts):
        at, of = pl.ds(i * some_rows, some_rows), pl.ds(i * some_cols, some_cols)
        fed_back = mm(ortho[at, :], right[...])
        sum_v[at, :] = (merged[at, :].astype(F32) - 0.05 * fed_back).astype(BF16)
        stores[2 * i + 1].start()
        loads[i].wait()
        update_v[:, of] = mm(o2[...], wall_v[:, of]).astype(BF16)
        stores[2 * i + 2].start()
    for store in stores:
        store.wait()


def shards(nz, ny, nx, flat_grad, flat_rows, momentum, basis):
    tile_rows, tile_cols = momentum.shape
    flat, cols = flat_grad.shape
    rank = basis.shape[1]
    n_col, n_row = nz * ny, nx * CORES
    piece = tile_cols // n_row
    half = tile_cols // CORES
    factor = math.sqrt(tile_rows * n_row * cols / rank)
    dma = pltpu.SemaphoreType.DMA
    any_space = pl.BlockSpec(memory_space=pl.ANY)
    vmem = pl.BlockSpec(memory_space=pltpu.VMEM)
    hbm = pl.BlockSpec(memory_space=pltpu.HBM)
    shape = jax.ShapeDtypeStruct
    merged, ortho, right, new_basis, o2, wall = pl.pallas_call(
        functools.partial(main_kernel, nz, ny, nx, factor),
        out_shape=[
            shape((tile_rows, tile_cols), BF16),
            shape((tile_rows, rank), BF16),
            shape((rank, tile_cols), BF16),
            shape((tile_cols, rank), F32),
            shape((flat, rank), BF16),
            shape((rank, cols), BF16),
        ],
        in_specs=[hbm, hbm, hbm, hbm],
        out_specs=[any_space, vmem, vmem, vmem, vmem, any_space],
        scratch_shapes=[
            pltpu.VMEM((tile_rows, tile_cols), BF16),
            pltpu.VMEM((tile_rows, tile_cols), BF16),
            pltpu.VMEM((tile_rows, tile_cols), BF16),
            pltpu.VMEM((tile_cols, tile_rows), BF16),
            pltpu.VMEM((tile_rows, tile_rows), BF16),
            pltpu.VMEM((tile_rows, tile_rows), BF16),
            pltpu.VMEM((1, flat), jnp.int32),
            pltpu.VMEM((n_col, 8, 128), jnp.int32),
            pltpu.VMEM((tile_cols, rank), BF16),
            pltpu.VMEM((tile_rows, rank), BF16),
            pltpu.VMEM(((n_col - 1) * flat, rank), BF16),
            pltpu.VMEM((tile_rows, rank), BF16),
            pltpu.VMEM((rank, rank), F32),
            pltpu.VMEM((rank, rank), F32),
            pltpu.VMEM((nx, rank // CORES, rank), F32),
            pltpu.VMEM((rank, rank), F32),
            pltpu.VMEM((half, rank), BF16),
            pltpu.VMEM((half, rank), BF16),
            pltpu.VMEM((half, rank), BF16),
            pltpu.VMEM(((nx - 1) * piece, rank), BF16),
            pltpu.VMEM((tile_cols, rank), BF16),
            pltpu.VMEM((tile_cols, rank), F32),
            pltpu.VMEM((n_col, 8, rank), F32),
            pltpu.VMEM((tile_cols, rank), F32),
            pltpu.VMEM((tile_rows, rank), BF16),
            pltpu.VMEM((rank, rank), F32),
            pltpu.VMEM((rank, rank), F32),
            pltpu.VMEM((rank, rank), F32),
            dma, dma,
            dma, dma,
            dma, dma((flat // ROUND,)),
            dma((CHUNKS,)), dma((CHUNKS,)), dma, dma, dma((CHUNKS,)), dma((CHUNKS,)),
            dma, dma, dma((2,)), dma((2,)), dma((2,)), dma((2,)), dma, dma((2, nx)),
            dma, dma((2, n_col)),
            dma, dma((2,)),
            dma((2,)), dma((2,)),
            dma((flat // ROUND,)),
            dma, dma,
        ],
        compiler_params=pltpu.CompilerParams(
            collective_id=0, has_side_effects=True, vmem_limit_bytes=42 * 1024 * 1024
        ),
        name="dion_main",
    )(flat_grad, flat_rows.reshape(1, flat), momentum, basis)

    parts = 8
    new_momentum, update, new_basis = pl.pallas_call(
        functools.partial(output_kernel, parts),
        out_shape=[
            shape((tile_rows, tile_cols), BF16),
            shape((flat, cols), BF16),
            shape((tile_cols, rank), F32),
        ],
        in_specs=[vmem, vmem, vmem, vmem, vmem, any_space],
        out_specs=[any_space, any_space, any_space],
        scratch_shapes=[
            pltpu.VMEM((rank, cols), BF16),
            pltpu.VMEM((tile_rows, tile_cols), BF16),
            pltpu.VMEM((flat, cols), BF16),
            dma((parts,)),
            dma((3, parts)),
        ],
        compiler_params=pltpu.CompilerParams(vmem_limit_bytes=44 * 1024 * 1024),
        name="dion_outputs",
    )(o2, ortho, right, merged, new_basis, wall)
    return new_momentum, new_basis, update


def solution(mesh):
    n_row, n_col = mesh.shape["row"], mesh.shape["col"]
    ny = math.isqrt(n_col)
    return jax.shard_map(
        functools.partial(shards, n_col // ny, ny, n_row // CORES),
        mesh=mesh,
        in_specs=(P(("row", "col"), None), P(("row", "col")), P("row", "col"), P("col", None)),
        out_specs=(P("row", "col"), P("col", None), P(("row", "col"), None)),
        check_vma=False,
    )
```

```python
import functools
import math

import jax
import jax.numpy as jnp
from jax import lax
from jax.experimental import pallas as pl
from jax.experimental.pallas import tpu as pltpu
from jax.sharding import PartitionSpec as P

ITERS = 4
CORES = 2
STEP = 32
ROUND = 32
CHUNKS = 3
MESH = pl.DeviceIdType.MESH
BF16 = jnp.bfloat16
F32 = jnp.float32
NN = (((1,), (0,)), ((), ()))
NT = (((1,), (1,)), ((), ()))
TN = (((0,), (0,)), ((), ()))


def mm(a, b, dims=NN):
    return lax.dot_general(a, b, dims, preferred_element_type=F32)


def split(a):
    high = a.astype(BF16)
    return high, (a - high.astype(F32)).astype(BF16)


def main_kernel(
    nz, ny, nx, factor,
    grad, slots_in, mom, basis,
    merged_out, ortho_out, right_out, basis_out, o2_out, wall,
    momv, recv, merged, turned, perm, perm_t, named_in, slots, current, rs_send, rs_recv, left, gram_own, gram_pair, gram_x, gram_all, w_send, w_pair, w_mid, w_recv, wag,
    w_sum, squares, rightf, ortho, amat, xmat, linv, mom_sem, out_sem, slot_s, slot_r, grad_s, grad_r,
    rs_s, rs_r, sq_s, sq_r, ag_s, ag_r, gram_s, gram_r, wrs_s, wrs_r, xrs_s, xrs_r, wag_s, wag_r, wall_s, wall_r, pair_s, pair_r,
    half_s, half_r, own_sem, last_s, last_r,
):
    row, col = lax.axis_index("row"), lax.axis_index("col")
    z, y = col // ny, col % ny
    x, core = row // CORES, row % CORES
    n_col, n_row = nz * ny, nx * CORES
    tile_rows, tile_cols = merged.shape
    rank = current.shape[1]
    flat = tile_rows // n_col
    rounds, per_round = flat // ROUND, n_col * ROUND
    group = flat * ny
    piece = tile_cols // n_row
    quarter = tile_cols // 4
    half = tile_cols // CORES
    offsets = [(dz, dy) for dz in range(nz) for dy in range(ny) if (dz, dy) != (0, 0)]
    offsets.sort(key=lambda o: (min(o[0], nz - o[0]) + min(o[1], ny - o[1]), max(o)))
    far_first = offsets[::-1]
    across = sorted(range(1, nx), key=lambda d: -min(d, nx - d))
    partner = x * CORES + (1 - core)

    def shifted(dz, dy):
        return lax.rem(z + dz, nz) * ny + lax.rem(y + dy, ny)

    def beside(dx):
        return lax.rem(x + dx, nx) * CORES + core

    def rows_at(index, size):
        return pl.ds(pl.multiple_of(index * size, size), size)

    def remote(src, dst, send, receive, to_row, to_col):
        return pltpu.make_async_remote_copy(
            src_ref=src, dst_ref=dst, send_sem=send, recv_sem=receive, device_id=(to_row, to_col), device_id_type=MESH
        )

    def await_recv(ref, sem):
        remote(ref, ref, sem, sem, partner, col).wait_recv()

    def await_send(ref, sem):
        remote(ref, ref, sem, sem, partner, col).wait_send()

    load = pltpu.make_async_copy(mom, momv, mom_sem)
    load.start()
    load_basis = pltpu.make_async_copy(basis, rightf, half_s.at[0])
    load_basis.start()
    load_slots = pltpu.make_async_copy(slots_in, named_in, half_s.at[1])
    load_slots.start()
    squares[...] = jnp.zeros_like(squares)

    barrier = pltpu.get_barrier_semaphore()
    for dz, dy in offsets:
        pl.semaphore_signal(barrier, inc=1, device_id=(row, shifted(dz, dy)), device_id_type=MESH)
    for dx in range(1, nx):
        pl.semaphore_signal(barrier, inc=1, device_id=(beside(dx), col), device_id_type=MESH)
    pl.semaphore_signal(barrier, inc=1, device_id=(partner, col), device_id_type=MESH)
    pl.semaphore_wait(barrier, n_col - 1 + nx)

    slots[col] = jnp.zeros((8, 128), jnp.int32)
    load_slots.wait()
    slots[col, 0:1, 0:flat] = named_in[...]
    for dz, dy in offsets:
        remote(slots.at[col], slots.at[col], slot_s, slot_r, row, shifted(dz, dy)).start()

    def columns_of(c):
        return pl.ds(pl.multiple_of(c * tile_cols, 128), tile_cols)

    def row_of(r, c):
        return pl.ds(pl.multiple_of(r * per_round + c * ROUND, ROUND), ROUND)

    own = []
    for r in range(rounds):
        taken = pl.ds(r * ROUND, ROUND)
        for dz, dy in offsets:
            to = shifted(dz, dy)
            remote(
                grad.at[taken, columns_of(to)], recv.at[row_of(r, col), :], grad_s, grad_r.at[r], row, to
            ).start()
        own.append(
            pltpu.make_async_copy(grad.at[taken, columns_of(col)], recv.at[row_of(r, col), :], own_sem.at[r])
        )
        own[r].start()

    load_basis.wait()
    current[...] = rightf[...].astype(BF16)
    await_recv(slots.at[pl.ds(0, n_col - 1)], slot_r)
    await_send(slots.at[pl.ds(0, n_col - 1)], slot_s)

    def fill_perm(c, _):
        named = jnp.broadcast_to(slots[c][0:1, :], (128, 128)).T - row * tile_rows
        lanes = lax.broadcasted_iota(jnp.int32, (ROUND, 128), 1)
        for r in range(rounds):
            part = named[r * ROUND : (r + 1) * ROUND]
            for t in range(tile_rows // 128):
                perm[row_of(r, c), t * 128 : (t + 1) * 128] = jnp.where(part == lanes + t * 128, 1.0, 0.0).astype(BF16)
        return 0

    lax.fori_loop(0, n_col, fill_perm, 0)
    load.wait()

    wide = 256
    n_wide, rest = tile_cols // wide, tile_cols % wide

    def permute(target, one, source, at):
        block = one[at, :]

        def part(t, _):
            cols = rows_at(t, wide)
            target[at, cols] = mm(block, source[:, cols]).astype(BF16)
            return 0

        lax.fori_loop(0, n_wide, part, 0)
        if rest:
            cols = pl.ds(n_wide * wide, rest)
            target[at, cols] = mm(block, source[:, cols]).astype(BF16)

    def permute_group(g, _):
        permute(merged, perm, momv, rows_at(g, group))
        return 0

    lax.fori_loop(0, nz, permute_group, 0)

    def turn_perm(t, _):
        cols = rows_at(t, 128)
        perm_t[cols, :] = perm[:, cols].T
        return 0

    lax.fori_loop(0, tile_rows // 128, turn_perm, 0)

    for r in range(rounds):
        begin = r * per_round
        own[r].wait()
        await_recv(recv.at[pl.ds(0, (n_col - 1) * ROUND), :], grad_r.at[r])

        def add(i, _, begin=begin):
            at = pl.ds(pl.multiple_of(begin + i * ROUND, ROUND), ROUND)
            merged[at, :] = (merged[at, :].astype(F32) + recv[at, :].astype(F32)).astype(BF16)
            return 0

        lax.fori_loop(0, n_col, add, 0)

        def turn(t, _, begin=begin):
            cols = rows_at(t, 128)
            turned[cols, begin : begin + per_round] = merged[begin : begin + per_round, cols].T
            return 0

        lax.fori_loop(0, tile_cols // 128, turn, 0)
    await_send(recv.at[pl.ds(0, (n_col - 1) * flat), :], grad_s)

    lane = lax.broadcasted_iota(jnp.int32, (STEP, rank), 1)
    sub = lax.broadcasted_iota(jnp.int32, (STEP, rank), 0)

    def eliminate(b, _, last=False):
        start = b * STEP
        at = rows_at(b, STEP)
        a, v = amat[at, :], xmat[at, :]
        spread = [
            jnp.broadcast_to(jnp.sum(jnp.where(lane == start + k, a, 0.0), axis=1, keepdims=True), (STEP, rank))
            for k in range(STEP)
        ]
        inverse = jnp.ones((STEP, rank), F32)
        for k in range(STEP):
            one_over = 1.0 / jnp.broadcast_to(spread[k][k : k + 1, :], (STEP, rank))
            inverse = jnp.where(sub == k, one_over, inverse)
            if k < STEP - 1:
                ratio = jnp.where(sub > k, spread[k] * one_over, 0.0)
                a = a - ratio * jnp.broadcast_to(a[k : k + 1, :], (STEP, rank))
                v = v - ratio * jnp.broadcast_to(v[k : k + 1, :], (STEP, rank))
                for j in range(k + 1, STEP):
                    spread[j] = spread[j] - ratio * jnp.broadcast_to(spread[j][k : k + 1, :], (STEP, rank))
        linv[at, :] = v * jnp.sqrt(inverse)
        if last:
            return 0
        scaled = jnp.where(lane >= start + STEP, a * inverse, 0.0)
        change = lax.dot_general(
            scaled,
            jnp.concatenate([a, v], axis=1),
            TN,
            precision=lax.Precision.HIGHEST,
            preferred_element_type=F32,
        )
        amat[...] -= change[:, :rank]
        xmat[...] -= change[:, rank:]
        return 0

    steps = rank // STEP
    chunk, share = tile_rows // CHUNKS, flat // CHUNKS
    restored = tile_rows // (2 * ITERS)

    def share_of(h, c):
        return pl.ds(pl.multiple_of(h * chunk + c * share, share), share)

    def others(ref, h):
        return ref.at[pl.ds(h * (n_col - 1) * share, (n_col - 1) * share), :]

    gram_half = rank // CORES

    sizes = [(piece // 2 + 15) // 16 * 16]
    sizes.append(piece - sizes[0])
    PARTS = (0, 1)

    def half_rows(e, c):
        return pl.ds(pl.multiple_of(e * n_row * sizes[0] + c * nx * sizes[e], 16), nx * sizes[e])

    def held(e, xc):
        return pl.ds(pl.multiple_of(e * n_row * sizes[0] + (core * nx + xc) * sizes[e], 16), sizes[e])

    def mid_rows(e, xc):
        return pl.ds(pl.multiple_of(e * nx * sizes[0] + xc * sizes[e], 16), sizes[e])

    def mid_part(e):
        return pl.ds(e * nx * sizes[0], nx * sizes[e])

    def recv_rows(e, i):
        return pl.ds(e * (nx - 1) * sizes[0] + i * sizes[e], sizes[e])

    def recv_part(e):
        return pl.ds(e * (nx - 1) * sizes[0], (nx - 1) * sizes[e])


    def iterate(k, _):
        for h in range(CHUNKS):
            at = slice(h * chunk, (h + 1) * chunk)
            rs_send[at, :] = mm(merged[at, :], current[...]).astype(BF16)
            for i, (dz, dy) in enumerate(far_first):
                to = shifted(dz, dy)
                slot = pl.ds((h * (n_col - 1) + i) * share, share)
                remote(rs_send.at[share_of(h, to), :], rs_recv.at[slot, :], rs_s.at[h], rs_r.at[h], row, to).start()
            if h == 0:
                for dz, dy in offsets:
                    to = shifted(dz, dy)
                    remote(squares.at[col, pl.ds(0, 1)], squares.at[col, pl.ds(0, 1)], sq_s, sq_r, row, to).start()
        permute(momv, perm_t, merged, rows_at(2 * k, restored))
        await_recv(squares.at[pl.ds(0, n_col - 1), pl.ds(0, 1)], sq_r)
        norm = jnp.sqrt(jnp.sum(squares[:, 0:1, :], axis=0) + 1e-06)
        scale = 1.0 / jnp.where(k == 0, jnp.ones_like(norm), norm)
        for h in range(CHUNKS):
            await_recv(others(rs_recv, h), rs_r.at[h])
            total = rs_send[share_of(h, col), :].astype(F32)
            for i in range(n_col - 1):
                begin = (h * (n_col - 1) + i) * share
                total = total + rs_recv[begin : begin + share, :].astype(F32)
            left[share_of(h, col), :] = (total * scale).astype(BF16)
            for dz, dy in far_first:
                ours = left.at[share_of(h, col), :]
                remote(ours, ours, ag_s.at[h], ag_r.at[h], row, shifted(dz, dy)).start()
        xmat[...] = jnp.where(
            lax.broadcasted_iota(jnp.int32, (rank, rank), 0) == lax.broadcasted_iota(jnp.int32, (rank, rank), 1), 1.0, 0.0
        )
        await_send(squares.at[pl.ds(0, n_col - 1), pl.ds(0, 1)], sq_s)
        for h in range(CHUNKS):
            await_send(others(rs_recv, h), rs_s.at[h])

        for h in range(CHUNKS):
            at = slice(h * chunk, (h + 1) * chunk)
            await_recv(others(rs_recv, h), ag_r.at[h])
            gram_part = mm(left[at, :], left[at, :], TN)
            gram_own[...] = gram_part if h == 0 else gram_own[...] + gram_part
            if h < CHUNKS - 1:
                w_part = mm(turned[:, at], left[at, :])
                w_sum[...] = w_part if h == 0 else w_sum[...] + w_part
        final = slice((CHUNKS - 1) * chunk, CHUNKS * chunk)
        to_pair = remote(gram_own, gram_pair, gram_s, gram_r, partner, col)
        to_pair.start()
        w_to_pair = []
        for e in PARTS:
            at = half_rows(e, 1 - core)
            here = mid_part(e)
            w_send[here, :] = (w_sum[at, :] + mm(turned[at, final], left[final, :])).astype(BF16)
            w_to_pair.append(
                remote(w_send.at[here, :], w_pair.at[here, :], wrs_s.at[e], wrs_r.at[e], partner, col)
            )
            w_to_pair[e].start()
        await_recv(gram_pair, gram_r)
        gram_rows = rows_at(core, gram_half)
        gram_x[x] = gram_own[gram_rows, :] + gram_pair[gram_rows, :]
        for dx in across:
            remote(gram_x.at[x], gram_x.at[x], half_s.at[0], half_r.at[0], beside(dx), col).start()
        for e in PARTS:
            at = half_rows(e, core)
            here = mid_part(e)
            own_half = w_sum[at, :] + mm(turned[at, final], left[final, :])
            await_recv(w_pair.at[here, :], wrs_r.at[e])
            w_mid[here, :] = (own_half + w_pair[here, :].astype(F32)).astype(BF16)
            for dx in across:
                to = lax.rem(x + dx, nx)
                slot = w_recv.at[recv_rows(e, dx - 1), :]
                remote(w_mid.at[mid_rows(e, to), :], slot, xrs_s.at[e], xrs_r.at[e], beside(dx), col).start()
        for h in range(CHUNKS):
            await_send(others(rs_recv, h), ag_s.at[h])
        permute(momv, perm_t, merged, rows_at(2 * k + 1, restored))
        await_recv(gram_x.at[pl.ds(0, nx - 1)], half_r.at[0])
        gram = gram_x[0]
        for d in range(1, nx):
            gram = gram + gram_x[d]
        gram_all[gram_rows, :] = gram
        halves = remote(gram_all.at[gram_rows, :], gram_all.at[gram_rows, :], half_s.at[1], half_r.at[1], partner, col)
        halves.start()
        for e in PARTS:
            await_recv(w_recv.at[recv_part(e), :], xrs_r.at[e])
            total = w_mid[mid_rows(e, x), :].astype(F32)
            for d in range(nx - 1):
                total = total + w_recv[recv_rows(e, d), :].astype(F32)
            wag[held(e, x), :] = total.astype(BF16)
            ours = wag.at[held(e, x), :]
            for dx in across:
                remote(ours, ours, wag_s, wag_r.at[e, x], beside(dx), col).start()
            remote(ours, ours, pair_s, pair_r.at[e], partner, col).start()
            if e == 0:
                await_recv(gram_all.at[gram_rows, :], half_r.at[1])
                amat[...] = gram_all[...]
                lax.fori_loop(0, 1, eliminate, 0)
        lax.fori_loop(1, 2, eliminate, 0)
        for e in PARTS:
            for dx in range(1, nx):
                xc = lax.rem(x + dx, nx)
                theirs = wag.at[held(e, xc), :]
                await_recv(theirs, wag_r.at[e, xc])
                remote(theirs, theirs, pair_s, pair_r.at[e], partner, col).start()
            if e == 0:
                lax.fori_loop(2, steps - 1, eliminate, 0)
        eliminate(steps - 1, 0, last=True)

        high, low = split(linv[...])

        def right_of(at):
            part = mm(wag[at, :], high, NT) + mm(wag[at, :], low, NT)
            rightf[at, :] = part
            current[at, :] = part.astype(BF16)
            return jnp.sum(part * part, axis=0, keepdims=True)

        near_sum = right_of(half_rows(0, core)) + right_of(half_rows(1, core))
        to_pair.wait_send()
        for e in PARTS:
            w_to_pair[e].wait_send()
            await_send(w_recv.at[recv_part(e), :], xrs_s.at[e])
        await_send(gram_x.at[pl.ds(0, nx - 1)], half_s.at[0])
        halves.wait_send()
        await_send(w_recv, wag_s)
        far_sum = []
        for e in PARTS:
            await_recv(w_pair.at[mid_part(e), :], pair_r.at[e])
            far_sum.append(right_of(half_rows(e, 1 - core)))
        summed = near_sum + (far_sum[0] + far_sum[1])
        await_send(w_pair, pair_s)
        squares[col] = jnp.broadcast_to(summed, (8, rank))
        return 0

    lax.fori_loop(0, ITERS, iterate, 0)

    store = pltpu.make_async_copy(momv, merged_out, mom_sem)
    store.start()

    def turn_right(t, _):
        at = rows_at(t, 128)
        right_out[:, at] = current[at, :].T
        return 0

    lax.fori_loop(0, tile_cols // 128, turn_right, 0)

    rank_part = rank // 4

    def cut(c, p):
        return pl.ds(pl.multiple_of((core * 2 + p) * rank_part, rank_part), rank_part), columns_of(c)

    def cut_half(c, p, h):
        size = rank_part // 2
        return pl.ds(pl.multiple_of((core * 2 + p) * rank_part + h * size, size), size), columns_of(c)

    def along(p, a, b):
        return shifted(a, b) if p == 0 else shifted(b, a)

    def send_own(p, to):
        part, cols = cut(col, p)
        remote(right_out.at[part, :], wall.at[part, cols], wall_s, wall_r.at[p, col], row, to).start()

    def send_part(at, p, c, to):
        remote(wall.at[at], wall.at[at], wall_s, wall_r.at[p, c], row, to).start()

    def to_partner(p, c):
        remote(wall.at[cut(c, p)], wall.at[cut(c, p)], last_s, last_r, partner, col).start()

    near = (1, ny - 1) if ny == 4 else tuple(range(1, ny))
    far = (2,) if ny == 4 else ()

    def pass_near(p, c, axis, d):
        if far:
            to = along(p, ny - d, 0) if axis == 0 else along(p, 0, ny - d)
            send_part(cut_half(c, p, 0 if d == 1 else 1), p, c, to)

    def spread_second(p, c):
        for d in near:
            send_part(cut(c, p), p, c, along(p, 0, d))

    def arrived(p, a, b):
        c = along(p, a, b)
        await_recv(wall.at[cut(c, p)], wall_r.at[p, c])
        return c

    write = pltpu.make_async_copy(right_out, wall.at[:, columns_of(col)], out_sem)
    write.start()
    for p in range(2):
        for d in near:
            send_own(p, along(p, d, 0))
    for p in range(2):
        for d in near:
            send_own(p, along(p, 0, d))
    for dz, dy in offsets:
        remote(squares.at[col, pl.ds(0, 1)], squares.at[col, pl.ds(0, 1)], sq_s, sq_r, row, shifted(dz, dy)).start()
    high, low = split(linv[...])
    ortho[...] = (mm(left[...], high, NT) + mm(left[...], low, NT)).astype(BF16)
    for a in near:
        for p in range(2):
            c = arrived(p, a, 0)
            pass_near(p, c, 0, a)
            spread_second(p, c)
            to_partner(p, c)
    for b in near:
        for p in range(2):
            c = arrived(p, 0, b)
            pass_near(p, c, 1, b)
            to_partner(p, c)
    for a in far:
        for p in range(2):
            c = arrived(p, a, 0)
            spread_second(p, c)
            to_partner(p, c)
    await_recv(squares.at[pl.ds(0, n_col - 1), pl.ds(0, 1)], sq_r)
    await_send(squares.at[pl.ds(0, n_col - 1), pl.ds(0, 1)], sq_s)
    norm = jnp.sqrt(jnp.sum(squares[:, 0:1, :], axis=0) + 1e-06)
    basis_out[...] = rightf[...] / norm
    for r in range(rounds):
        o2_out[r * ROUND : (r + 1) * ROUND, :] = (ortho[row_of(r, col), :].astype(F32) * (factor / norm)).astype(BF16)
    for a in near:
        for b in near:
            for p in range(2):
                c = arrived(p, a, b)
                pass_near(p, c, 1, b)
                to_partner(p, c)
    ortho_out[...] = mm(perm_t[...], ortho[...]).astype(BF16)
    for b in far:
        for p in range(2):
            to_partner(p, arrived(p, 0, b))
    for a in far:
        for b in near:
            for p in range(2):
                c = arrived(p, a, b)
                pass_near(p, c, 1, b)
                to_partner(p, c)
    for a in near + far:
        for b in far:
            for p in range(2):
                to_partner(p, arrived(p, a, b))
    most = pl.ds(0, 2 * rank_part), pl.ds(0, (n_col - 1) * tile_cols)
    await_recv(wall.at[most], last_r)
    await_send(wall.at[most], last_s)
    await_send(wall.at[most], wall_s)
    store.wait()
    write.wait()


def output_kernel(
    parts, o2, ortho, right, merged, basis, wall, new_momentum, update, new_basis, wall_v, sum_v, update_v, in_sem, out_sem
):
    flat, cols = update.shape
    tile_rows = merged.shape[0]
    some_rows, some_cols = tile_rows // parts, cols // parts
    loads, stores = [], [pltpu.make_async_copy(basis, new_basis, out_sem.at[2, 0])]
    for i in range(parts):
        at, of = pl.ds(i * some_rows, some_rows), pl.ds(i * some_cols, some_cols)
        loads.append(pltpu.make_async_copy(wall.at[:, of], wall_v.at[:, of], in_sem.at[i]))
        stores.append(pltpu.make_async_copy(sum_v.at[at, :], new_momentum.at[at, :], out_sem.at[0, i]))
        stores.append(pltpu.make_async_copy(update_v.at[:, of], update.at[:, of], out_sem.at[1, i]))
    for load in loads:
        load.start()
    stores[0].start()
    for i in range(parts):
        at, of = pl.ds(i * some_rows, some_rows), pl.ds(i * some_cols, some_cols)
        fed_back = mm(ortho[at, :], right[...])
        sum_v[at, :] = (merged[at, :].astype(F32) - 0.05 * fed_back).astype(BF16)
        stores[2 * i + 1].start()
        loads[i].wait()
        update_v[:, of] = mm(o2[...], wall_v[:, of]).astype(BF16)
        stores[2 * i + 2].start()
    for store in stores:
        store.wait()


def shards(nz, ny, nx, flat_grad, flat_rows, momentum, basis):
    tile_rows, tile_cols = momentum.shape
    flat, cols = flat_grad.shape
    rank = basis.shape[1]
    n_col, n_row = nz * ny, nx * CORES
    piece = tile_cols // n_row
    half = tile_cols // CORES
    factor = math.sqrt(tile_rows * n_row * cols / rank)
    dma = pltpu.SemaphoreType.DMA
    any_space = pl.BlockSpec(memory_space=pl.ANY)
    vmem = pl.BlockSpec(memory_space=pltpu.VMEM)
    hbm = pl.BlockSpec(memory_space=pltpu.HBM)
    shape = jax.ShapeDtypeStruct
    merged, ortho, right, new_basis, o2, wall = pl.pallas_call(
        functools.partial(main_kernel, nz, ny, nx, factor),
        out_shape=[
            shape((tile_rows, tile_cols), BF16),
            shape((tile_rows, rank), BF16),
            shape((rank, tile_cols), BF16),
            shape((tile_cols, rank), F32),
            shape((flat, rank), BF16),
            shape((rank, cols), BF16),
        ],
        in_specs=[hbm, hbm, hbm, hbm],
        out_specs=[any_space, vmem, vmem, vmem, vmem, any_space],
        scratch_shapes=[
            pltpu.VMEM((tile_rows, tile_cols), BF16),
            pltpu.VMEM((tile_rows, tile_cols), BF16),
            pltpu.VMEM((tile_rows, tile_cols), BF16),
            pltpu.VMEM((tile_cols, tile_rows), BF16),
            pltpu.VMEM((tile_rows, tile_rows), BF16),
            pltpu.VMEM((tile_rows, tile_rows), BF16),
            pltpu.VMEM((1, flat), jnp.int32),
            pltpu.VMEM((n_col, 8, 128), jnp.int32),
            pltpu.VMEM((tile_cols, rank), BF16),
            pltpu.VMEM((tile_rows, rank), BF16),
            pltpu.VMEM(((n_col - 1) * flat, rank), BF16),
            pltpu.VMEM((tile_rows, rank), BF16),
            pltpu.VMEM((rank, rank), F32),
            pltpu.VMEM((rank, rank), F32),
            pltpu.VMEM((nx, rank // CORES, rank), F32),
            pltpu.VMEM((rank, rank), F32),
            pltpu.VMEM((half, rank), BF16),
            pltpu.VMEM((half, rank), BF16),
            pltpu.VMEM((half, rank), BF16),
            pltpu.VMEM(((nx - 1) * piece, rank), BF16),
            pltpu.VMEM((tile_cols, rank), BF16),
            pltpu.VMEM((tile_cols, rank), F32),
            pltpu.VMEM((n_col, 8, rank), F32),
            pltpu.VMEM((tile_cols, rank), F32),
            pltpu.VMEM((tile_rows, rank), BF16),
            pltpu.VMEM((rank, rank), F32),
            pltpu.VMEM((rank, rank), F32),
            pltpu.VMEM((rank, rank), F32),
            dma, dma,
            dma, dma,
            dma, dma((flat // ROUND,)),
            dma((CHUNKS,)), dma((CHUNKS,)), dma, dma, dma((CHUNKS,)), dma((CHUNKS,)),
            dma, dma, dma((2,)), dma((2,)), dma((2,)), dma((2,)), dma, dma((2, nx)),
            dma, dma((2, n_col)),
            dma, dma((2,)),
            dma((2,)), dma((2,)),
            dma((flat // ROUND,)),
            dma, dma,
        ],
        compiler_params=pltpu.CompilerParams(
            collective_id=0, has_side_effects=True, vmem_limit_bytes=42 * 1024 * 1024
        ),
        name="dion_main",
    )(flat_grad, flat_rows.reshape(1, flat), momentum, basis)

    parts = 8
    new_momentum, update, new_basis = pl.pallas_call(
        functools.partial(output_kernel, parts),
        out_shape=[
            shape((tile_rows, tile_cols), BF16),
            shape((flat, cols), BF16),
            shape((tile_cols, rank), F32),
        ],
        in_specs=[vmem, vmem, vmem, vmem, vmem, any_space],
        out_specs=[any_space, any_space, any_space],
        scratch_shapes=[
            pltpu.VMEM((rank, cols), BF16),
            pltpu.VMEM((tile_rows, tile_cols), BF16),
            pltpu.VMEM((flat, cols), BF16),
            dma((parts,)),
            dma((3, parts)),
        ],
        compiler_params=pltpu.CompilerParams(vmem_limit_bytes=44 * 1024 * 1024),
        name="dion_outputs",
    )(o2, ortho, right, merged, new_basis, wall)
    return new_momentum, new_basis, update


def solution(mesh):
    n_row, n_col = mesh.shape["row"], mesh.shape["col"]
    ny = math.isqrt(n_col)
    return jax.shard_map(
        functools.partial(shards, n_col // ny, ny, n_row // CORES),
        mesh=mesh,
        in_specs=(P(("row", "col"), None), P(("row", "col")), P("row", "col"), P("col", None)),
        out_specs=(P("row", "col"), P("col", None), P(("row", "col"), None)),
        check_vma=False,
    )
```
